128 devices in a mesh: ctx: 16 (over x_lo, z, core), fsdp: 8 (over y, x_hi).
Axes of the slice: x: 4 (x_hi: 2, x_lo: 2; x = x_hi * 2 + x_lo), y: 4, z: 4, core: 2. Of those that a mesh axis runs over, the one named last changes fastest.
Arguments:
- tokens: bfloat16 [8, 2048, 1024], P('fsdp', 'ctx'), may hold values from -6 to 6
- cotangent: bfloat16 [8, 2048, 1024], P('fsdp', 'ctx'), may hold values from -6 to 6
- places: int32 [8, 2048], P('fsdp'), may hold values from 0 to 2047, as said below
- doc_split: int32 [8], P('fsdp'), may hold values from 512 to 1536
- w_query: bfloat16 [1024, 1024], P('fsdp'), may hold values from -0.1875 to 0.1875
- w_key: bfloat16 [1024, 512], P('fsdp'), may hold values from -0.1875 to 0.1875
- w_value: bfloat16 [1024, 512], P('fsdp'), may hold values from -0.1875 to 0.1875
- w_out: bfloat16 [1024, 1024], P('fsdp'), may hold values from -1 to 1
- w_gate: bfloat16 [1024, 4608], P('fsdp'), may hold values from -0.1875 to 0.1875
- w_up: bfloat16 [1024, 4608], P('fsdp'), may hold values from -0.1875 to 0.1875
- w_down: bfloat16 [4608, 1024], P('fsdp'), may hold values from -0.09375 to 0.09375
- norm_attn: bfloat16 [1024], P('fsdp'), may hold values from 0.099609375 to 1.8984375
- norm_ffn: bfloat16 [1024], P('fsdp'), may hold values from 0.099609375 to 1.8984375
- norm_query: bfloat16 [64], P('fsdp'), may hold values from 0.099609375 to 1.8984375
- norm_key: bfloat16 [64], P('fsdp'), may hold values from 0.099609375 to 1.8984375
Outputs:
- layer_out: bfloat16 [8, 2048, 1024], P('fsdp', 'ctx')
- grad_tokens: bfloat16 [8, 2048, 1024], P('fsdp', 'ctx')
- grad_w_query: float32 [1024, 1024], P('fsdp')
- grad_w_key: float32 [1024, 512], P('fsdp')
- grad_w_value: float32 [1024, 512], P('fsdp')
- grad_w_out: float32 [1024, 1024], P('fsdp')
- grad_w_gate: float32 [1024, 4608], P('fsdp')
- grad_w_up: float32 [1024, 4608], P('fsdp')
- grad_w_down: float32 [4608, 1024], P('fsdp')
- grad_norm_attn: float32 [1024], P('fsdp')
- grad_norm_ffn: float32 [1024], P('fsdp')
- grad_norm_query: float32 [64], P('fsdp')
- grad_norm_key: float32 [64], P('fsdp')
The draws below stay inside these ranges and needn't reach their ends.
Inputs may be any that keep to these rules, and one draw needn't show every extreme that they name: In each row the places are a permutation of 0 to 2047 cut into 32 blocks of 64 places; the tokens of each device of ctx hold, in order, one block b and the block 31 - b, b drawn per row. `doc_split`: places below it form the first document of the row, the rest the second.
All inputs are finite; a program needn't handle non-finite values.
Results may differ from the reference program's by a relative error of at most 0.03.
Values may be sent and summed in bfloat16 or wider, within the bound.
No kernel may reach another device: no remote copies, remote signals or barrier semaphores. Data moves between devices by JAX's collectives and lax.ppermute only.
A program may use at most 192 MiB of HBM per device.

```python
import jax
import jax.numpy as jnp
from jax import lax

D = 1024
H = 16
KVH = 8
HD = 64
FF = 4608
TOK_DEV = 128
GROUPS = 8
LEN = 2048


def draw_places(key, part):
    key = jax.random.fold_in(key, 11)
    block_count = LEN // TOK_DEV
    half_block = TOK_DEV // 2
    group_keys = jax.random.split(key, GROUPS)
    orders = jax.vmap(lambda sub_key: jax.random.permutation(sub_key, block_count))(group_keys)
    offsets = jnp.arange(half_block)
    early_rows = orders[:, :, None] * half_block + offsets[None, None, :]
    late_rows = (2 * block_count - 1 - orders)[:, :, None] * half_block + offsets[None, None, :]
    return jnp.concatenate([early_rows, late_rows], axis=2).reshape(GROUPS, LEN).astype(jnp.int32)


def with_ends(entries, key, smallest, high):
    longest = entries.shape.index(max(entries.shape))
    spots = []
    for shift in (0, 1):
        where = [jax.random.randint(jax.random.fold_in(key, axis), (), 0, length) for axis, length in enumerate(entries.shape)]
        where[longest] = (where[longest] + shift) % entries.shape[longest]
        spots.append(tuple(where))
    return entries.at[spots[0]].set(smallest).at[spots[1]].set(high)


def block_scale(rng, shape, cuts, low, high):
    loudness, own = 1.0, jax.random.fold_in(rng, 6)
    for axis_at, parts in cuts:
        heights = jnp.exp(jax.random.uniform(jax.random.fold_in(own, axis_at), (parts,), jnp.float32, low / len(cuts), high / len(cuts)))
        loudness = loudness * jnp.repeat(heights, shape[axis_at] // parts).reshape([-1 if axis == axis_at else 1 for axis in range(len(shape))])
    return loudness


def normal_values(rng, shape, spread, most, shards=(), kind=jnp.bfloat16):
    values = spread * jax.random.normal(rng, shape, jnp.float32)
    if shards:
        values = values * block_scale(rng, shape, shards, -0.22, 0.18)
    return jnp.clip(values, -most, most).astype(kind)


def setup_inputs(seed: int = 0) -> dict:
    arg_keys = jax.random.split(jax.random.key(seed), 16)
    return {
        "tokens": normal_values(arg_keys[0], (GROUPS, LEN, D), 1.0, 6.0, ((0, 8), (1, 16))),
        "cotangent": normal_values(arg_keys[1], (GROUPS, LEN, D), 1.0, 6.0, ((0, 8), (1, 16))),
        "places": draw_places(jax.random.fold_in(arg_keys[15], 71), 0),
        "doc_split": with_ends(jax.random.randint(arg_keys[3], (GROUPS,), LEN // 4, 3 * LEN // 4 + 1), jax.random.fold_in(arg_keys[3], 1), LEN // 4, (3 * LEN // 4 + 1) - 1).astype(jnp.int32),
        "w_query": normal_values(arg_keys[4], (D, H * HD), D ** -0.5, 0.1875, ((0, 8),)),
        "w_key": normal_values(arg_keys[5], (D, KVH * HD), D ** -0.5, 0.1875, ((0, 8),)),
        "w_value": normal_values(arg_keys[6], (D, KVH * HD), D ** -0.5, 0.1875, ((0, 8),)),
        "w_out": normal_values(arg_keys[7], (H * HD, D), (H * HD // 32) ** -0.5, 1.0, ((0, 8),)),
        "w_gate": normal_values(arg_keys[8], (D, FF), D ** -0.5, 0.1875, ((0, 8),)),
        "w_up": normal_values(arg_keys[9], (D, FF), D ** -0.5, 0.1875, ((0, 8),)),
        "w_down": normal_values(arg_keys[10], (FF, D), FF ** -0.5, 0.09375, ((0, 8),)),
        "norm_attn": jnp.clip(1.0 + 0.18 * jax.random.normal(arg_keys[11], (D,), jnp.float32), 0.099609375, 1.8984375).astype(jnp.bfloat16),
        "norm_ffn": jnp.clip(1.0 + 0.18 * jax.random.normal(arg_keys[12], (D,), jnp.float32), 0.099609375, 1.8984375).astype(jnp.bfloat16),
        "norm_query": jnp.clip(1.0 + 0.18 * jax.random.normal(arg_keys[13], (HD,), jnp.float32), 0.099609375, 1.8984375).astype(jnp.bfloat16),
        "norm_key": jnp.clip(1.0 + 0.18 * jax.random.normal(arg_keys[14], (HD,), jnp.float32), 0.099609375, 1.8984375).astype(jnp.bfloat16),
    }


EPS = 1e-05
THETA = 1000000.0

@jax.custom_vjp
def low(v):
    return lax.optimization_barrier(v.astype(jnp.bfloat16)).astype(jnp.float32)

@jax.custom_vjp
def low_back(v):
    return v

def low_keep(v):
    return (low(v), None)

def low_pass(kept, grad):
    return (grad,)

def back_keep(v):
    return (v, None)

def back_low(kept, grad):
    return (low(grad),)
low.defvjp(low_keep, low_pass)
low_back.defvjp(back_keep, back_low)

def precise_dot(left_side, right_side):
    return jnp.dot(left_side, right_side, precision=lax.Precision.HIGHEST, preferred_element_type=jnp.float32)

def rms_scale(values, scales):
    return values * lax.rsqrt(lax.optimization_barrier(jnp.mean(values * values, axis=-1, keepdims=True)) + EPS) * scales

def rotate(values, cosine_table, sine_table):
    half_width = values.shape[-1] // 2
    turned = jnp.concatenate([-values[..., half_width:], values[..., :half_width]], axis=-1)
    return values * cosine_table + turned * sine_table

def angle_tables(places_row, split_at):
    second_doc = places_row >= split_at
    position = (places_row - jnp.where(second_doc, split_at, 0)).astype(jnp.float32)
    freq_index = jnp.arange(HD // 2).astype(jnp.float32)
    inv_freq = THETA ** (-2.0 * freq_index / HD)
    phases = position[:, None] * inv_freq[None, :]
    phases = jnp.concatenate([phases, phases], axis=-1)
    return (jnp.cos(phases)[:, None, :], jnp.sin(phases)[:, None, :], second_doc)

def group_forward(inputs_f, weights, cosine_table, sine_table, visible):
    w_query, w_key, w_value, w_out, w_gate, w_up, w_down, gain_attn, gain_ffn, gain_query, gain_key = weights
    row_count = inputs_f.shape[0]
    per_group = H // KVH
    normed_in = low(rms_scale(inputs_f, gain_attn))
    queries = low_back(precise_dot(normed_in, w_query)).reshape(row_count, H, HD)
    key_proj = low_back(precise_dot(normed_in, w_key)).reshape(row_count, KVH, HD)
    value_proj = low(low_back(precise_dot(normed_in, w_value))).reshape(row_count, KVH, HD)
    queries = low_back(low(rotate(rms_scale(queries, gain_query), cosine_table, sine_table)))
    key_proj = low_back(low(rotate(rms_scale(key_proj, gain_key), cosine_table, sine_table)))
    queries = queries.reshape(row_count, KVH, per_group, HD).transpose(1, 2, 0, 3)
    key_proj = key_proj.transpose(1, 0, 2)
    value_proj = value_proj.transpose(1, 0, 2)
    score_scale = HD ** (-0.5)

    def one_head(head_items):
        q_head, k_head, v_head = head_items
        raw_scores = jnp.einsum('gqd,kd->gqk', q_head, k_head, precision=lax.Precision.HIGHEST) * score_scale
        scores = low_back(jnp.where(visible[None], raw_scores, -1e+30))
        row_max = lax.optimization_barrier(jnp.max(scores, axis=-1, keepdims=True))
        exponent = jnp.exp(scores - row_max)
        probability = low(exponent / lax.optimization_barrier(jnp.sum(exponent, axis=-1, keepdims=True)))
        return jnp.einsum('gqk,kd->gqd', probability, v_head, precision=lax.Precision.HIGHEST)
    head_outputs = lax.map(jax.checkpoint(one_head), (queries, key_proj, value_proj))
    attended = head_outputs.transpose(2, 0, 1, 3).reshape(row_count, H * HD)
    attended = low_back(low(attended))
    residual = inputs_f + low_back(precise_dot(attended, w_out))
    normed_mid = low(rms_scale(residual, gain_ffn))
    gate_proj = low_back(precise_dot(normed_mid, w_gate))
    up_proj = low_back(precise_dot(normed_mid, w_up))
    hidden_act = low(jax.nn.silu(gate_proj) * up_proj)
    return residual + precise_dot(hidden_act, w_down)

def reference(tokens, cotangent, places, doc_split, w_query, w_key, w_value, w_out, w_gate, w_up, w_down, norm_attn, norm_ffn, norm_query, norm_key):
    weights = tuple((weight.astype(jnp.float32) for weight in (w_query, w_key, w_value, w_out, w_gate, w_up, w_down, norm_attn, norm_ffn, norm_query, norm_key)))

    def group_step(totals, group_items):
        inputs_f, cot_rows, places_row, split_at = group_items
        cosine_table, sine_table, second_doc = angle_tables(places_row, split_at)
        visible = (second_doc[:, None] == second_doc[None, :]) & (places_row[None, :] <= places_row[:, None])

        def forward_fn(inputs_now, *weight_list):
            return group_forward(inputs_now, weight_list, cosine_table, sine_table, visible)
        result, pullback = jax.vjp(forward_fn, inputs_f, *weights)
        gradients = pullback(cot_rows)
        totals = tuple((total + update for total, update in zip(totals, gradients[1:])))
        return (totals, (result.astype(jnp.bfloat16), gradients[0].astype(jnp.bfloat16)))
    zero_grads = tuple((jnp.zeros(weight.shape, jnp.float32) for weight in weights))
    totals, (layer_out, input_grad) = lax.scan(group_step, zero_grads, (tokens.astype(jnp.float32), cotangent.astype(jnp.float32), places, doc_split))
    return (layer_out, input_grad, totals[0], totals[1], totals[2], totals[3], totals[4], totals[5], totals[6], totals[7], totals[8], totals[9], totals[10])
```

```python
import functools

import jax
import jax.numpy as jnp
import numpy as np
from jax import lax
from jax.experimental import pallas as pl
from jax.experimental.pallas import tpu as pltpu
from jax.sharding import Mesh
from jax.sharding import PartitionSpec as P

D = 1024
H = 16
KVH = 8
HD = 64
FF = 4608
TOK = 128
LEN = 2048
HALF = 1024
FSL = FF // 8
BLK = 64
EPS = 1e-05
THETA = 1000000.0
F32 = jnp.float32
BF16 = jnp.bfloat16
NA, NZ, NC, NY, NB = 2, 4, 2, 4, 2
CTX = ("a", "z", "c")
FS = ("y", "b")


def dot(left, right, dims=((1,), (0,))):
    return lax.dot_general(left, right, (dims, ((), ())), preferred_element_type=F32)


def shift(value, axis, size, step):
    return lax.ppermute(value, axis, [(i, (i + step) % size) for i in range(size)])


def swap(value, axis):
    return shift(value, axis, 2, 1)


def after(value, *earlier):
    return lax.optimization_barrier((value, earlier))[0]


def ring(own):
    return jnp.concatenate([own] + [shift(own, "z", NZ, step) for step in (1, 2, 3)], axis=0)


def both_cores(same):
    return jnp.concatenate([same, swap(same, "c")], axis=0)


def add_cores(mine, low, *earlier):
    return mine + after(swap(low, "c"), *earlier).astype(F32)


def add_ring(mine, *earlier):
    low = mine.astype(BF16)
    parts = [shift(low[step * TOK : (step + 1) * TOK], "z", NZ, -step) for step in (1, 2, 3)]
    if earlier:
        parts = after(parts, *earlier)
    total = mine[:TOK]
    for part in parts:
        total = total + part.astype(F32)
    return total


def heads_ring(own):
    return jnp.stack([own] + [shift(own, "z", NZ, step) for step in (1, 2, 3)])


def cross(value):
    pairs = [(m * 8 + j, j * 8 + m) for m in range(8) for j in range(8)]
    return lax.ppermute(value, ("z", "c", "y", "b"), pairs)


def fetch_shard(value):
    pairs = []
    for z, c, y, b in np.ndindex(NZ, NC, NY, NB):
        source = (((y + z) % 4 * 2 + b) * 4 + z) * 2 + c
        pairs.append((source, ((z * 2 + c) * 4 + y) * 2 + b))
    return lax.ppermute(value, ("z", "c", "y", "b"), pairs)


KC = 256


def sort_keys(kb_ref, own_ref, peer_ref, keys, values, values_one):
    for i in range(32):
        src = own_ref if i < 16 else peer_ref
        r = (i % 16) * BLK
        rows = pl.ds(pl.multiple_of(kb_ref[i] * BLK, BLK), BLK)
        block = src[r : r + BLK, :]
        keys[rows, :] = block[:, :HD]
        part = block[:, HD:]
        if values is not None:
            values[rows, :] = part
        if values_one is not None:
            values_one[rows, :] = jnp.concatenate([part, jnp.ones_like(part)], axis=1)


def key_range(p, split):
    first = jnp.where(p * BLK >= split, split // KC, 0)
    return first, (p * BLK) // KC + 1


def attention_forward_kernel(kb_ref, split_ref, q_ref, own_ref, peer_ref, out_ref, sum_ref, keys, values_one):
    sort_keys(kb_ref, own_ref, peer_ref, keys, None, values_one)
    split = split_ref[0]

    def one_block(i, _):
        p = kb_ref[i]
        rows = pl.ds(pl.multiple_of(i * BLK, BLK), BLK)
        q = jnp.concatenate([q_ref[0, rows, :], q_ref[1, rows, :]], axis=0)
        row_place = p * BLK + lax.rem(lax.broadcasted_iota(jnp.int32, (2 * BLK, KC), 0), BLK)
        start = jnp.where(row_place >= split, split, 0)
        col = lax.broadcasted_iota(jnp.int32, (2 * BLK, KC), 1)

        def one_chunk(ck, acc):
            at = pl.multiple_of(ck * KC, KC)
            s = dot(q, keys[pl.ds(at, KC), :], ((1,), (1,)))
            key_place = col + at
            seen = (key_place <= row_place) & (key_place >= start)
            e = jnp.where(seen, jnp.exp(s), 0.0).astype(BF16)
            return acc + dot(e, values_one[pl.ds(at, KC), :])

        lo, hi = key_range(p, split)
        acc = lax.fori_loop(lo, hi, one_chunk, jnp.zeros((2 * BLK, 2 * HD), F32))
        o = acc[:, :HD] / acc[:, HD:]
        out_ref[rows, :] = jnp.concatenate([o[:BLK], o[BLK:]], axis=1).astype(BF16)
        sum_ref[pl.ds(pl.multiple_of(i * 8, 8), 8), :] = acc.T[HD : HD + 8, :]
        return 0

    lax.fori_loop(0, 16, one_block, 0)


SMEM = pl.BlockSpec(memory_space=pltpu.SMEM)
VMEM = pl.BlockSpec(memory_space=pltpu.VMEM)


def attention_forward(blocks, split, queries, own, peer):
    return pl.pallas_call(
        attention_forward_kernel,
        out_shape=(
            jax.ShapeDtypeStruct((HALF, 2 * HD), BF16),
            jax.ShapeDtypeStruct((128, 128), F32),
        ),
        in_specs=[SMEM, SMEM, VMEM, VMEM, VMEM],
        out_specs=(VMEM, VMEM),
        scratch_shapes=[pltpu.VMEM((LEN, HD), BF16), pltpu.VMEM((LEN, 2 * HD), BF16)],
        compiler_params=pltpu.CompilerParams(vmem_limit_bytes=32 * 2**20),
        cost_estimate=pl.CostEstimate(flops=16 * 10**9, bytes_accessed=2 * 10**6, transcendentals=2 * 10**6),
    )(blocks, split, queries, own, peer)


def attention_backward_kernel(
    kb_ref, split_ref, q_ref, own_ref, peer_ref, att_ref, do_ref, sum_ref,
    dq_ref, down_ref, dpeer_ref, keys, values, keys_t, dk, dv,
):
    sort_keys(kb_ref, own_ref, peer_ref, keys, values, None)
    for i in range(LEN // KC):
        keys_t[:, i * KC : (i + 1) * KC] = keys[i * KC : (i + 1) * KC, :].T
    dk[...] = jnp.zeros_like(dk)
    dv[...] = jnp.zeros_like(dv)
    split = split_ref[0]

    def one_block(i, _):
        p = kb_ref[i]
        rows = pl.ds(pl.multiple_of(i * BLK, BLK), BLK)
        q = jnp.concatenate([q_ref[0, rows, :], q_ref[1, rows, :]], axis=0)
        pair = do_ref[rows, :]
        do = jnp.concatenate([pair[:, :HD], pair[:, HD:]], axis=0)
        prod = pair.astype(F32) * att_ref[rows, :].astype(F32)
        prod = jnp.concatenate([prod[:, :HD], prod[:, HD:]], axis=0)
        inner = jnp.sum(prod.T, axis=0, keepdims=True)
        inv = 1.0 / sum_ref[pl.ds(pl.multiple_of(i * 8, 8), 8), :][:1]
        row_place = p * BLK + lax.rem(lax.broadcasted_iota(jnp.int32, (KC, 2 * BLK), 1), BLK)
        start = jnp.where(row_place >= split, split, 0)
        col = lax.broadcasted_iota(jnp.int32, (KC, 2 * BLK), 0)

        def one_chunk(ck, dqt):
            at = pl.multiple_of(ck * KC, KC)
            here = pl.ds(at, KC)
            s = dot(keys[here, :], q, ((1,), (1,)))
            dp = dot(values[here, :], do, ((1,), (1,)))
            key_place = col + at
            seen = (key_place <= row_place) & (key_place >= start)
            prob = jnp.where(seen, jnp.exp(s), 0.0) * inv
            ds = (prob * (dp - inner)).astype(BF16)
            dv[here, :] += dot(prob.astype(BF16), do)
            dk[here, :] += dot(ds, q)
            return dqt + dot(keys_t[:, here], ds)

        lo, hi = key_range(p, split)
        dqt = lax.fori_loop(lo, hi, one_chunk, jnp.zeros((HD, 2 * BLK), F32))
        dq = (dqt.T * (HD ** -0.5)).astype(BF16)
        dq_ref[0, rows, :] = dq[:BLK]
        dq_ref[1, rows, :] = dq[BLK:]
        return 0

    lax.fori_loop(0, 16, one_block, 0)
    for i in range(32):
        rows = pl.ds(pl.multiple_of(kb_ref[i] * BLK, BLK), BLK)
        both = jnp.concatenate([dk[rows, :], dv[rows, :]], axis=1)
        r = (i % 16) * BLK
        if i < 16:
            down_ref[r : r + BLK, :] = both
        else:
            dpeer_ref[r : r + BLK, :] = both.astype(BF16)


def attention_backward(blocks, split, queries, own, peer, attended, grad, sums):
    return pl.pallas_call(
        attention_backward_kernel,
        out_shape=(
            jax.ShapeDtypeStruct((2, HALF, HD), BF16),
            jax.ShapeDtypeStruct((HALF, 2 * HD), F32),
            jax.ShapeDtypeStruct((HALF, 2 * HD), BF16),
        ),
        in_specs=[SMEM, SMEM] + [VMEM] * 6,
        out_specs=(VMEM, VMEM, VMEM),
        scratch_shapes=[
            pltpu.VMEM((LEN, HD), BF16),
            pltpu.VMEM((LEN, HD), BF16),
            pltpu.VMEM((HD, LEN), BF16),
            pltpu.VMEM((LEN, HD), F32),
            pltpu.VMEM((LEN, HD), F32),
        ],
        compiler_params=pltpu.CompilerParams(vmem_limit_bytes=32 * 2**20),
        cost_estimate=pl.CostEstimate(flops=20 * 10**9, bytes_accessed=4 * 10**6, transcendentals=2 * 10**6),
    )(blocks, split, queries, own, peer, attended, grad, sums)


def ffn_kernel(
    order_ref, x_ref, same_ref, other_ref, weights_ref, down_ref, cot_ref, gain_ref,
    h2_ref, d_gate_ref, d_up_ref, act_ref, dh2_mine_ref, dh2_low_ref, out_mine_ref, out_low_ref,
    y1_ref, gain_grad_ref, w_out, w_gate, w_up,
):
    i = pl.program_id(0)

    @pl.when(i == 0)
    def _():
        for k in range(8):
            rows = slice(k * 128, (k + 1) * 128)
            w_out[rows, :] = weights_ref[order_ref[k], :, :D]
            w_gate[rows, :] = weights_ref[k, :, D : D + FSL]
            w_up[rows, :] = weights_ref[k, :, D + 640 : D + 640 + FSL]
        gain_grad_ref[...] = jnp.zeros_like(gain_grad_ref)

    chunks = []
    for half in range(2):
        dc, dz = i // 2, (i % 2) * 2 + half
        parts = []
        for ref, core in ((same_ref, dc), (other_ref, 1 - dc)):
            for step in range(4):
                row = (core * 4 + (dz - step + 4) % 4) * TOK
                parts.append(ref[step, pl.ds(pl.multiple_of(row, TOK), TOK), :])
        chunks.append(jnp.concatenate(parts, axis=1))
    att = jnp.concatenate(chunks, axis=0)
    y1 = x_ref[...].astype(F32) + dot(att, w_out[...])
    r2 = lax.rsqrt(jnp.mean(y1 * y1, axis=1, keepdims=True) + EPS)
    n2 = y1 * r2
    h2 = (n2 * gain_ref[...]).astype(BF16)
    h2_ref[...] = h2

    @pl.when(i == 0)
    def _():
        y1_ref[...] = y1[:TOK]

    gate = dot(h2, w_gate[...])
    up = dot(h2, w_up[...])
    da = dot(cot_ref[...], down_ref[...], ((1,), (1,)))
    sg = 1.0 / (1.0 + jnp.exp(-gate))
    silu = gate * sg
    act = (silu * up).astype(BF16)
    d_up = (da * silu).astype(BF16)
    d_gate = (da * up * (sg * (1.0 + gate * (1.0 - sg)))).astype(BF16)
    act_ref[...] = act
    d_up_ref[...] = d_up
    d_gate_ref[...] = d_gate
    dh2 = dot(d_gate, w_gate[...], ((1,), (1,))) + dot(d_up, w_up[...], ((1,), (1,)))
    gain_grad_ref[...] += jnp.sum(dh2 * n2, axis=0, keepdims=True)
    out = dot(act, down_ref[...])

    @pl.when(i < 2)
    def _():
        dh2_mine_ref[...] = dh2
        out_mine_ref[...] = out

    @pl.when(i >= 2)
    def _():
        dh2_low_ref[...] = dh2.astype(BF16)
        out_low_ref[...] = out.astype(BF16)


def ffn(order, x, same, other, weights, down, cot, gain):
    rows = 256

    def whole(shape):
        return pl.BlockSpec(shape, lambda i: (0,) * len(shape))

    tokens = pl.BlockSpec((rows, D), lambda i: (i, 0))
    hidden = pl.BlockSpec((rows, FSL), lambda i: (i, 0))
    first = pl.BlockSpec((rows, D), lambda i: (jnp.minimum(i, 1), 0))
    last = pl.BlockSpec((rows, D), lambda i: (jnp.maximum(i - 2, 0), 0))
    return pl.pallas_call(
        ffn_kernel,
        grid=(HALF // rows,),
        in_specs=[
            SMEM, tokens, whole((4, HALF, 128)), whole((4, HALF, 128)),
            whole((8, 128, 2240)), whole((FSL, D)), tokens, whole((1, D)),
        ],
        out_specs=(tokens, hidden, hidden, hidden, first, last, first, last, whole((TOK, D)), whole((1, D))),
        out_shape=(
            jax.ShapeDtypeStruct((HALF, D), BF16),
            jax.ShapeDtypeStruct((HALF, FSL), BF16),
            jax.ShapeDtypeStruct((HALF, FSL), BF16),
            jax.ShapeDtypeStruct((HALF, FSL), BF16),
            jax.ShapeDtypeStruct((512, D), F32),
            jax.ShapeDtypeStruct((512, D), BF16),
            jax.ShapeDtypeStruct((512, D), F32),
            jax.ShapeDtypeStruct((512, D), BF16),
            jax.ShapeDtypeStruct((TOK, D), F32),
            jax.ShapeDtypeStruct((1, D), F32),
        ),
        scratch_shapes=[
            pltpu.VMEM((D, D), BF16),
            pltpu.VMEM((D, FSL), BF16),
            pltpu.VMEM((D, FSL), BF16),
        ],
        compiler_params=pltpu.CompilerParams(vmem_limit_bytes=48 * 2**20),
        cost_estimate=pl.CostEstimate(flops=11 * 10**9, bytes_accessed=24 * 10**6, transcendentals=10**6),
    )(order, x, same, other, weights, down, cot, gain)


def ffn_weights_kernel(h2_ref, cot_ref, d_gate_ref, d_up_ref, act_ref, out_ref):
    for k in range(4):
        columns = slice(k * 256, (k + 1) * 256)
        h2 = h2_ref[:, columns]
        cot = cot_ref[:, columns]
        for n, (left, right) in enumerate(((h2, d_gate_ref), (h2, d_up_ref), (cot, act_ref))):
            block = dot(left, right[...], ((0,), (0,))).astype(BF16)
            for i in range(4):
                out_ref[4 * k + i, n] = block[i * 64 : (i + 1) * 64]


def ffn_weights(h2, cot, d_gate, d_up, act):
    return pl.pallas_call(
        ffn_weights_kernel,
        in_specs=[VMEM] * 5,
        out_specs=VMEM,
        out_shape=jax.ShapeDtypeStruct((16, 3, 64, FSL), BF16),
        compiler_params=pltpu.CompilerParams(vmem_limit_bytes=40 * 2**20),
        cost_estimate=pl.CostEstimate(flops=4 * 10**9, bytes_accessed=11 * 10**6, transcendentals=0),
    )(h2, cot, d_gate, d_up, act)


def assemble_ffn_kernel(in_ref, gate_ref, up_ref, down_ref):
    for a in range(2):
        rows = pl.ds(a * 64, 64)
        gate_ref[rows, :] = jnp.concatenate([in_ref[a, 0, 0], in_ref[a, 1, 0]], axis=1).astype(F32)
        up_ref[rows, :] = jnp.concatenate([in_ref[a, 0, 1], in_ref[a, 1, 1]], axis=1).astype(F32)
    for i in range(2):
        block = jnp.concatenate([in_ref[0, i, 2], in_ref[1, i, 2]], axis=0).astype(F32)
        block = jnp.concatenate([block, jnp.zeros((128, 64), F32)], axis=1)
        down_ref[:, i * 128 : (i + 1) * 128] = block.T[:FSL]


def assemble_ffn(gathered):
    return pl.pallas_call(
        assemble_ffn_kernel,
        grid=(4,),
        in_specs=[pl.BlockSpec((2, 2, 3, 64, FSL), lambda i: (0, i, 0, 0, 0))],
        out_specs=(
            pl.BlockSpec((TOK, 2 * FSL), lambda i: (0, i)),
            pl.BlockSpec((TOK, 2 * FSL), lambda i: (0, i)),
            pl.BlockSpec((FSL, 256), lambda i: (0, i)),
        ),
        out_shape=(
            jax.ShapeDtypeStruct((TOK, FF), F32),
            jax.ShapeDtypeStruct((TOK, FF), F32),
            jax.ShapeDtypeStruct((FSL, D), F32),
        ),
        compiler_params=pltpu.CompilerParams(vmem_limit_bytes=32 * 2**20),
        cost_estimate=pl.CostEstimate(flops=0, bytes_accessed=11 * 10**6, transcendentals=0),
    )(gathered)


def assemble_attention_kernel(in_ref, query_ref, key_ref, value_ref, out_ref, gain_ref):
    for pair in range(4):
        for i in range(2):
            m = 2 * pair + i
            both = jnp.concatenate([in_ref[0, m, :64], in_ref[1, m, :64]], axis=0).astype(F32)
            query_ref[:, m * 128 : (m + 1) * 128] = both[:, :128]
            out_ref[:, m * 128 : (m + 1) * 128] = both[:, 256:].T
        for lo, ref in ((128, key_ref), (192, value_ref)):
            for a in range(2):
                ref[a * 64 : (a + 1) * 64, pair * 128 : (pair + 1) * 128] = jnp.concatenate(
                    [in_ref[a, 2 * pair + i, :64, lo : lo + 64] for i in range(2)], axis=1
                ).astype(F32)
    for a in range(2):
        gain_ref[a] = sum(in_ref[a, m, 64:].astype(F32) for m in range(8))


def assemble_attention(gathered):
    outs = pl.pallas_call(
        assemble_attention_kernel,
        out_shape=(
            jax.ShapeDtypeStruct((TOK, D), F32),
            jax.ShapeDtypeStruct((TOK, KVH * HD), F32),
            jax.ShapeDtypeStruct((TOK, KVH * HD), F32),
            jax.ShapeDtypeStruct((TOK, D), F32),
            jax.ShapeDtypeStruct((2, 16, 384), F32),
        ),
        in_specs=[VMEM],
        out_specs=(VMEM,) * 5,
        compiler_params=pltpu.CompilerParams(vmem_limit_bytes=32 * 2**20),
        cost_estimate=pl.CostEstimate(flops=0, bytes_accessed=3 * 10**6, transcendentals=0),
    )(gathered)
    return outs[:4] + (outs[4][:, 0, :],)


def rotate(values, cosine, sine):
    half = HD // 2
    turned = jnp.concatenate([-values[..., half:], values[..., :half]], axis=-1)
    return values * cosine + turned * sine


def unrotate(grads, cosine, sine):
    half = HD // 2
    scaled = grads * sine
    turned = jnp.concatenate([scaled[..., half:], -scaled[..., :half]], axis=-1)
    return grads * cosine + turned


def inv_rms(values):
    return lax.rsqrt(jnp.mean(values * values, axis=-1, keepdims=True) + EPS)


def norm_back(grads, normed, scale):
    return scale * (grads - normed * jnp.mean(grads * normed, axis=-1, keepdims=True))


def per_device(
    tokens, cotangent, places, doc_split,
    w_query, w_key, w_value, w_out, w_gate, w_up, w_down,
    norm_attn, norm_ffn, norm_query, norm_key,
):
    a, z, c = lax.axis_index("a"), lax.axis_index("z"), lax.axis_index("c")
    m = z * 2 + c
    own_tokens, own_cot = tokens[0], cotangent[0]

    gains = jnp.concatenate([norm_attn, norm_ffn, norm_query, norm_key, jnp.zeros((240,), BF16)])
    gains = jnp.concatenate([gains.reshape(2, 256), jnp.zeros((14, 256), BF16)], axis=0)
    qkv_own = jnp.concatenate(
        [
            lax.dynamic_slice_in_dim(w_query, m * 128, 128, 1),
            lax.dynamic_slice_in_dim(w_key, m * 64, 64, 1),
            lax.dynamic_slice_in_dim(w_value, m * 64, 64, 1),
        ],
        axis=1,
    )
    qkv_own = jnp.concatenate([qkv_own, gains], axis=0)
    qkv_all = lax.all_to_all(
        jnp.broadcast_to(qkv_own[None], (8, 144, 256)), FS, split_axis=0, concat_axis=0, tiled=True
    )
    x_same, w_down_m = after((ring(own_tokens), fetch_shard(w_down)))
    x_low = both_cores(x_same)
    w_qkv = qkv_all[:, :128].reshape(D, 256)
    gain_parts = qkv_all[:, 128:130].reshape(8, 512).astype(F32)
    gain_attn = gain_parts[:, :128].reshape(D)
    gain_ffn = gain_parts[:, 128:256].reshape(D)
    gain_query = gain_parts[:, 256:264].reshape(HD)
    gain_key = gain_parts[:, 264:272].reshape(HD)

    wide_own = jnp.concatenate(
        [
            w_out,
            lax.dynamic_slice_in_dim(w_gate, m * FSL, FSL, 1),
            jnp.zeros((TOK, 64), BF16),
            lax.dynamic_slice_in_dim(w_up, m * FSL, FSL, 1),
        ],
        axis=1,
    )
    wide = lax.all_gather(after(wide_own, qkv_all), FS, axis=0)

    block_of = places[0].reshape(32, BLK)[:, 0] // BLK
    wanted = []
    for half in (a, 1 - a):
        for dc in range(2):
            for dz in range(4):
                device = half * 8 + ((z - dz) % 4) * 2 + (c ^ dc)
                wanted += [device * 2, device * 2 + 1]
    wanted = jnp.stack(wanted)
    blocks = jnp.sum(
        jnp.where(wanted[:, None] == jnp.arange(32)[None, :], block_of[None, :], 0), axis=1
    ).astype(jnp.int32)
    place = (blocks[:16, None] * BLK + jnp.arange(BLK)[None, :]).reshape(HALF)
    split = doc_split[0]
    position = (place - jnp.where(place >= split, split, 0)).astype(F32)
    inv_freq = THETA ** (-2.0 * jnp.arange(HD // 2).astype(F32) / HD)
    phases = position[:, None] * inv_freq[None, :]
    phases = jnp.concatenate([phases, phases], axis=-1)
    cosine, sine = jnp.cos(phases)[None], jnp.sin(phases)[None]

    x = x_low.astype(F32)
    r1 = inv_rms(x)
    n1 = x * r1
    h1 = (n1 * gain_attn).astype(BF16)
    heads = jnp.einsum(
        "td,hde->hte", h1, w_qkv.reshape(D, 4, HD).transpose(1, 0, 2), preferred_element_type=F32
    )
    qp, kp, v_low = heads[:2], heads[2:3], heads[3].astype(BF16)
    rq, rk = inv_rms(qp), inv_rms(kp)
    qn, kn = qp * rq, kp * rk
    q_rot = rotate(qn * gain_query, cosine, sine).astype(BF16)
    k_rot = rotate(kn * gain_key, cosine, sine).astype(BF16)
    q_scaled = q_rot * jnp.asarray(HD ** -0.5, BF16)
    kv_own = jnp.concatenate([k_rot[0], v_low], axis=1)
    kv_peer = swap(kv_own, "a")
    cot_same = ring(after(own_cot, kv_own))
    attended, sums = attention_forward(blocks, doc_split, q_scaled, kv_own, kv_peer)

    heads_same = heads_ring(attended)
    heads_same, cot_same = after((heads_same, cot_same))
    heads_other = swap(heads_same, "c")
    cot = both_cores(cot_same)
    order = jnp.stack(
        [((z - dz) % 4) * 2 + (c ^ dc) for dc in range(2) for dz in range(4)]
    ).astype(jnp.int32)
    h2, d_gate, d_up, act, dh2_mine, dh2_low, out_mine, out_low, own_y1, grad_gain_ffn = ffn(
        order, x_low, heads_same, heads_other, wide, w_down_m, cot, gain_ffn[None]
    )

    dh2_same = add_cores(dh2_mine, dh2_low)
    ffn_terms = ffn_weights(h2, cot, d_gate, d_up, act)
    ffn_got = lax.all_to_all(ffn_terms, ("y", "b", "a"), split_axis=0, concat_axis=0, tiled=True)
    dh2 = add_ring(dh2_same, ffn_terms)
    own_r2 = inv_rms(own_y1)
    own_n2 = own_y1 * own_r2
    dy1 = own_cot.astype(F32) + norm_back(dh2 * gain_ffn, own_n2, own_r2)
    dz_low = dy1.astype(BF16)
    dz_same = ring(dz_low)
    dz = both_cores(dz_same)
    out_same = add_cores(out_mine, after(out_low, dz_same))

    w_out_m = lax.dynamic_index_in_dim(wide, m, 0, keepdims=False)[:, :D]
    d_att = dot(dz, w_out_m, ((1,), (1,))).astype(BF16)
    out_terms = dot(dz, attended, ((0,), (0,)))
    ffn_piece = jnp.sum(after(ffn_got, dz_same).astype(F32), axis=0).astype(BF16)
    ffn_piece = jnp.concatenate([ffn_piece[:2], cross(ffn_piece[2])[None]], axis=0)
    ffn_all = lax.all_gather(ffn_piece, CTX, axis=0).reshape(2, 8, 3, 64, FSL)
    d_att = after(d_att, out_terms, out_same, ffn_piece)
    dq_rot, dkv_own, dkv_peer = attention_backward(
        blocks, doc_split, q_scaled, kv_own, kv_peer, attended, d_att, sums
    )
    layer_out = (own_y1 + add_ring(out_same)).astype(BF16)
    dkv_own, layer_out = after((dkv_own, layer_out))
    dkv = dkv_own + swap(dkv_peer, "a").astype(F32)
    dk_rot, dv_low = dkv[None, :, :HD].astype(BF16).astype(F32), dkv[:, HD:].astype(BF16)
    dqn = unrotate(dq_rot.astype(F32), cosine, sine)
    dkn = unrotate(dk_rot, cosine, sine)
    grad_gain_query = jnp.sum(dqn * qn, axis=(0, 1))
    grad_gain_key = jnp.sum(dkn * kn, axis=(0, 1))
    dqp = norm_back(dqn * gain_query, qn, rq).astype(BF16)
    dkp = norm_back(dkn * gain_key, kn, rk).astype(BF16)
    dqkv = jnp.concatenate([dqp[0], dqp[1], dkp[0], dv_low], axis=1)
    dh1_part = dot(dqkv, w_qkv, ((1,), (1,)))
    grad_gain_attn = jnp.sum(dh1_part * n1, axis=0)
    attn_terms = jnp.concatenate([dot(h1, dqkv, ((0,), (0,))), out_terms], axis=1)
    gain_terms = jnp.concatenate(
        [
            grad_gain_attn.reshape(8, 128),
            grad_gain_ffn.reshape(8, 128),
            grad_gain_query.reshape(8, 8),
            grad_gain_key.reshape(8, 8),
        ],
        axis=1,
    ).reshape(8, 2, 1, 136)
    gain_terms = jnp.pad(gain_terms, ((0, 0), (0, 0), (0, 15), (0, 384 - 136)))
    terms = jnp.concatenate([attn_terms.reshape(8, 2, 64, 384), gain_terms], axis=2)
    terms = terms.astype(BF16).reshape(8, 2, 80, 384).reshape(16, 80, 384)
    dh1_same = add_cores(dh1_part[:512], dh1_part[512:].astype(BF16), terms)
    dh1 = add_ring(dh1_same)
    grad_tokens = (dy1 + norm_back(dh1 * gain_attn, n1[:TOK], r1[:TOK])).astype(BF16)
    got = lax.all_to_all(terms, ("y", "b", "a"), split_axis=0, concat_axis=0, tiled=True)
    piece = jnp.sum(after(got, dh1_same).astype(F32), axis=0).astype(BF16)
    piece = jnp.concatenate([piece[:, :256], cross(piece[:, 256:])], axis=1)
    piece, grad_tokens = after((piece, grad_tokens))
    gathered = lax.all_gather(piece, CTX, axis=0)
    grad_query, grad_key, grad_value, grad_out, gain_sum = assemble_attention(gathered.reshape(2, 8, 80, 384))
    gain_sum = gain_sum[:, :136].reshape(272)
    grad_gate, grad_up, grad_down = assemble_ffn(ffn_all)
    return (
        layer_out[None],
        grad_tokens[None],
        grad_query,
        grad_key,
        grad_value,
        grad_out,
        grad_gate,
        grad_up,
        grad_down,
        gain_sum[:128],
        gain_sum[128:256],
        gain_sum[256:264],
        gain_sum[264:],
    )


def solution(mesh):
    fine = Mesh(mesh.devices.reshape(NA, NZ, NC, NY, NB), CTX + FS)
    rows = P(FS, CTX, None)
    shard = P(FS, None)
    in_specs = (rows, rows, shard, P(FS)) + (shard,) * 7 + (P(FS),) * 4
    out_specs = (rows, rows) + (shard,) * 7 + (P(FS),) * 4
    return jax.shard_map(
        per_device, mesh=fine, in_specs=in_specs, out_specs=out_specs, check_vma=False
    )
```

```python
import functools

import jax
import jax.numpy as jnp
import numpy as np
from jax import lax
from jax.experimental import pallas as pl
from jax.experimental.pallas import tpu as pltpu
from jax.sharding import Mesh
from jax.sharding import PartitionSpec as P

D = 1024
H = 16
KVH = 8
HD = 64
FF = 4608
TOK = 128
LEN = 2048
HALF = 1024
FSL = FF // 8
BLK = 64
EPS = 1e-05
THETA = 1000000.0
F32 = jnp.float32
BF16 = jnp.bfloat16
NA, NZ, NC, NY, NB = 2, 4, 2, 4, 2
CTX = ("a", "z", "c")
FS = ("y", "b")


def dot(left, right, dims=((1,), (0,))):
    return lax.dot_general(left, right, (dims, ((), ())), preferred_element_type=F32)


def shift(value, axis, size, step):
    return lax.ppermute(value, axis, [(i, (i + step) % size) for i in range(size)])


def swap(value, axis):
    return shift(value, axis, 2, 1)


def after(value, *earlier):
    return lax.optimization_barrier((value, earlier))[0]


def ring(own):
    return jnp.concatenate([own] + [shift(own, "z", NZ, step) for step in (1, 2, 3)], axis=0)


def both_cores(same):
    return jnp.concatenate([same, swap(same, "c")], axis=0)


def add_cores(mine, low, *earlier):
    return mine + after(swap(low, "c"), *earlier).astype(F32)


def add_ring(mine, *earlier):
    low = mine.astype(BF16)
    parts = [shift(low[step * TOK : (step + 1) * TOK], "z", NZ, -step) for step in (1, 2, 3)]
    if earlier:
        parts = after(parts, *earlier)
    total = mine[:TOK]
    for part in parts:
        total = total + part.astype(F32)
    return total


def heads_ring(own):
    return jnp.stack([own] + [shift(own, "z", NZ, step) for step in (1, 2, 3)])


def cross(value):
    pairs = [(m * 8 + j, j * 8 + m) for m in range(8) for j in range(8)]
    return lax.ppermute(value, ("z", "c", "y", "b"), pairs)


def fetch_shard(value):
    pairs = []
    for z, c, y, b in np.ndindex(NZ, NC, NY, NB):
        source = (((y + z) % 4 * 2 + b) * 4 + z) * 2 + c
        pairs.append((source, ((z * 2 + c) * 4 + y) * 2 + b))
    return lax.ppermute(value, ("z", "c", "y", "b"), pairs)


KC = 256


def sort_keys(kb_ref, own_ref, peer_ref, keys, values, values_one):
    for i in range(32):
        src = own_ref if i < 16 else peer_ref
        r = (i % 16) * BLK
        rows = pl.ds(pl.multiple_of(kb_ref[i] * BLK, BLK), BLK)
        block = src[r : r + BLK, :]
        keys[rows, :] = block[:, :HD]
        part = block[:, HD:]
        if values is not None:
            values[rows, :] = part
        if values_one is not None:
            values_one[rows, :] = jnp.concatenate([part, jnp.ones_like(part)], axis=1)


def key_range(p, split):
    first = jnp.where(p * BLK >= split, split // KC, 0)
    return first, (p * BLK) // KC + 1


def attention_forward_kernel(kb_ref, split_ref, q_ref, own_ref, peer_ref, out_ref, sum_ref, keys, values_one):
    sort_keys(kb_ref, own_ref, peer_ref, keys, None, values_one)
    split = split_ref[0]

    def one_block(i, _):
        p = kb_ref[i]
        rows = pl.ds(pl.multiple_of(i * BLK, BLK), BLK)
        q = jnp.concatenate([q_ref[0, rows, :], q_ref[1, rows, :]], axis=0)
        row_place = p * BLK + lax.rem(lax.broadcasted_iota(jnp.int32, (2 * BLK, KC), 0), BLK)
        start = jnp.where(row_place >= split, split, 0)
        col = lax.broadcasted_iota(jnp.int32, (2 * BLK, KC), 1)

        def one_chunk(ck, acc):
            at = pl.multiple_of(ck * KC, KC)
            s = dot(q, keys[pl.ds(at, KC), :], ((1,), (1,)))
            key_place = col + at
            seen = (key_place <= row_place) & (key_place >= start)
            e = jnp.where(seen, jnp.exp(s), 0.0).astype(BF16)
            return acc + dot(e, values_one[pl.ds(at, KC), :])

        lo, hi = key_range(p, split)
        acc = lax.fori_loop(lo, hi, one_chunk, jnp.zeros((2 * BLK, 2 * HD), F32))
        o = acc[:, :HD] / acc[:, HD:]
        out_ref[rows, :] = jnp.concatenate([o[:BLK], o[BLK:]], axis=1).astype(BF16)
        sum_ref[pl.ds(pl.multiple_of(i * 8, 8), 8), :] = acc.T[HD : HD + 8, :]
        return 0

    lax.fori_loop(0, 16, one_block, 0)


SMEM = pl.BlockSpec(memory_space=pltpu.SMEM)
VMEM = pl.BlockSpec(memory_space=pltpu.VMEM)


def attention_forward(blocks, split, queries, own, peer):
    return pl.pallas_call(
        attention_forward_kernel,
        out_shape=(
            jax.ShapeDtypeStruct((HALF, 2 * HD), BF16),
            jax.ShapeDtypeStruct((128, 128), F32),
        ),
        in_specs=[SMEM, SMEM, VMEM, VMEM, VMEM],
        out_specs=(VMEM, VMEM),
        scratch_shapes=[pltpu.VMEM((LEN, HD), BF16), pltpu.VMEM((LEN, 2 * HD), BF16)],
        compiler_params=pltpu.CompilerParams(vmem_limit_bytes=32 * 2**20),
        cost_estimate=pl.CostEstimate(flops=5 * 10**8, bytes_accessed=2 * 10**6, transcendentals=0),
    )(blocks, split, queries, own, peer)


def attention_backward_kernel(
    kb_ref, split_ref, q_ref, own_ref, peer_ref, att_ref, do_ref, sum_ref,
    dq_ref, down_ref, dpeer_ref, keys, values, keys_t, dk, dv,
):
    sort_keys(kb_ref, own_ref, peer_ref, keys, values, None)
    for i in range(LEN // KC):
        keys_t[:, i * KC : (i + 1) * KC] = keys[i * KC : (i + 1) * KC, :].T
    dk[...] = jnp.zeros_like(dk)
    dv[...] = jnp.zeros_like(dv)
    split = split_ref[0]

    def one_block(i, _):
        p = kb_ref[i]
        rows = pl.ds(pl.multiple_of(i * BLK, BLK), BLK)
        q = jnp.concatenate([q_ref[0, rows, :], q_ref[1, rows, :]], axis=0)
        pair = do_ref[rows, :]
        do = jnp.concatenate([pair[:, :HD], pair[:, HD:]], axis=0)
        prod = pair.astype(F32) * att_ref[rows, :].astype(F32)
        prod = jnp.concatenate([prod[:, :HD], prod[:, HD:]], axis=0)
        inner = jnp.sum(prod.T, axis=0, keepdims=True)
        inv = 1.0 / sum_ref[pl.ds(pl.multiple_of(i * 8, 8), 8), :][:1]
        row_place = p * BLK + lax.rem(lax.broadcasted_iota(jnp.int32, (KC, 2 * BLK), 1), BLK)
        start = jnp.where(row_place >= split, split, 0)
        col = lax.broadcasted_iota(jnp.int32, (KC, 2 * BLK), 0)

        def one_chunk(ck, dqt):
            at = pl.multiple_of(ck * KC, KC)
            here = pl.ds(at, KC)
            s = dot(keys[here, :], q, ((1,), (1,)))
            dp = dot(values[here, :], do, ((1,), (1,)))
            key_place = col + at
            seen = (key_place <= row_place) & (key_place >= start)
            prob = jnp.where(seen, jnp.exp(s), 0.0) * inv
            ds = (prob * (dp - inner)).astype(BF16)
            dv[here, :] += dot(prob.astype(BF16), do)
            dk[here, :] += dot(ds, q)
            return dqt + dot(keys_t[:, here], ds)

        lo, hi = key_range(p, split)
        dqt = lax.fori_loop(lo, hi, one_chunk, jnp.zeros((HD, 2 * BLK), F32))
        dq = (dqt.T * (HD ** -0.5)).astype(BF16)
        dq_ref[0, rows, :] = dq[:BLK]
        dq_ref[1, rows, :] = dq[BLK:]
        return 0

    lax.fori_loop(0, 16, one_block, 0)
    for i in range(32):
        rows = pl.ds(pl.multiple_of(kb_ref[i] * BLK, BLK), BLK)
        both = jnp.concatenate([dk[rows, :], dv[rows, :]], axis=1)
        r = (i % 16) * BLK
        if i < 16:
            down_ref[r : r + BLK, :] = both
        else:
            dpeer_ref[r : r + BLK, :] = both.astype(BF16)


def attention_backward(blocks, split, queries, own, peer, attended, grad, sums):
    return pl.pallas_call(
        attention_backward_kernel,
        out_shape=(
            jax.ShapeDtypeStruct((2, HALF, HD), BF16),
            jax.ShapeDtypeStruct((HALF, 2 * HD), F32),
            jax.ShapeDtypeStruct((HALF, 2 * HD), BF16),
        ),
        in_specs=[SMEM, SMEM] + [VMEM] * 6,
        out_specs=(VMEM, VMEM, VMEM),
        scratch_shapes=[
            pltpu.VMEM((LEN, HD), BF16),
            pltpu.VMEM((LEN, HD), BF16),
            pltpu.VMEM((HD, LEN), BF16),
            pltpu.VMEM((LEN, HD), F32),
            pltpu.VMEM((LEN, HD), F32),
        ],
        compiler_params=pltpu.CompilerParams(vmem_limit_bytes=32 * 2**20),
        cost_estimate=pl.CostEstimate(flops=5 * 10**8, bytes_accessed=4 * 10**6, transcendentals=0),
    )(blocks, split, queries, own, peer, attended, grad, sums)


def ffn_kernel(
    order_ref, x_ref, x_other_ref, same_ref, other_ref, weights_ref, down_ref, cot_ref, cot_other_ref, gain_ref,
    h2_ref, d_gate_ref, d_up_ref, act_ref, dh2_mine_ref, dh2_low_ref, out_mine_ref, out_low_ref,
    y1_ref, gain_grad_ref, w_out, w_gate, w_up,
):
    i = pl.program_id(0)

    @pl.when(i == 0)
    def _():
        for k in range(8):
            rows = slice(k * 128, (k + 1) * 128)
            w_out[rows, :] = weights_ref[order_ref[k], :, :D]
            w_gate[rows, :] = weights_ref[k, :, D : D + FSL]
            w_up[rows, :] = weights_ref[k, :, D + 640 : D + 640 + FSL]
        gain_grad_ref[...] = jnp.zeros_like(gain_grad_ref)

    chunks = []
    for half in range(2):
        dc, dz = i // 2, (i % 2) * 2 + half
        parts = []
        for ref, core in ((same_ref, dc), (other_ref, 1 - dc)):
            for step in range(4):
                row = (core * 4 + (dz - step + 4) % 4) * TOK
                parts.append(ref[step, pl.ds(pl.multiple_of(row, TOK), TOK), :])
        chunks.append(jnp.concatenate(parts, axis=1))
    att = jnp.concatenate(chunks, axis=0)
    x = jnp.where(i < 2, x_ref[...], x_other_ref[...]).astype(F32)
    y1 = x + dot(att, w_out[...])
    r2 = lax.rsqrt(jnp.mean(y1 * y1, axis=1, keepdims=True) + EPS)
    n2 = y1 * r2
    h2 = (n2 * gain_ref[...]).astype(BF16)
    h2_ref[...] = h2

    @pl.when(i == 0)
    def _():
        y1_ref[...] = y1[:TOK]

    gate = dot(h2, w_gate[...])
    up = dot(h2, w_up[...])
    cot = jnp.where(i < 2, cot_ref[...], cot_other_ref[...])
    da = dot(cot, down_ref[...], ((1,), (1,)))
    sg = 1.0 / (1.0 + jnp.exp(-gate))
    silu = gate * sg
    act = (silu * up).astype(BF16)
    d_up = (da * silu).astype(BF16)
    d_gate = (da * up * (sg * (1.0 + gate * (1.0 - sg)))).astype(BF16)
    act_ref[...] = act
    d_up_ref[...] = d_up
    d_gate_ref[...] = d_gate
    dh2 = dot(d_gate, w_gate[...], ((1,), (1,))) + dot(d_up, w_up[...], ((1,), (1,)))
    gain_grad_ref[...] += jnp.sum(dh2 * n2, axis=0, keepdims=True)
    out = dot(act, down_ref[...])

    @pl.when(i < 2)
    def _():
        dh2_mine_ref[...] = dh2
        out_mine_ref[...] = out

    @pl.when(i >= 2)
    def _():
        dh2_low_ref[...] = dh2.astype(BF16)
        out_low_ref[...] = out.astype(BF16)


def ffn(order, x, x_other, same, other, weights, down, cot, cot_other, gain):
    rows = 256

    tokens = pl.BlockSpec((rows, D), lambda i: (i, 0))
    hidden = pl.BlockSpec((rows, FSL), lambda i: (i, 0))
    first = pl.BlockSpec((rows, D), lambda i: (jnp.minimum(i, 1), 0))
    last = pl.BlockSpec((rows, D), lambda i: (jnp.maximum(i - 2, 0), 0))
    return pl.pallas_call(
        ffn_kernel,
        grid=(HALF // rows,),
        in_specs=[
            SMEM, first, last, whole((4, HALF, 128)), whole((4, HALF, 128)),
            whole((8, 128, 2240)), whole((FSL, D)), first, last, whole((1, D)),
        ],
        out_specs=(tokens, hidden, hidden, hidden, first, last, first, last, whole((TOK, D)), whole((1, D))),
        out_shape=(
            jax.ShapeDtypeStruct((HALF, D), BF16),
            jax.ShapeDtypeStruct((HALF, FSL), BF16),
            jax.ShapeDtypeStruct((HALF, FSL), BF16),
            jax.ShapeDtypeStruct((HALF, FSL), BF16),
            jax.ShapeDtypeStruct((512, D), F32),
            jax.ShapeDtypeStruct((512, D), BF16),
            jax.ShapeDtypeStruct((512, D), F32),
            jax.ShapeDtypeStruct((512, D), BF16),
            jax.ShapeDtypeStruct((TOK, D), F32),
            jax.ShapeDtypeStruct((1, D), F32),
        ),
        scratch_shapes=[
            pltpu.VMEM((D, D), BF16),
            pltpu.VMEM((D, FSL), BF16),
            pltpu.VMEM((D, FSL), BF16),
        ],
        compiler_params=pltpu.CompilerParams(vmem_limit_bytes=48 * 2**20),
        cost_estimate=pl.CostEstimate(flops=11 * 10**9, bytes_accessed=24 * 10**6, transcendentals=10**6),
    )(order, x, x_other, same, other, weights, down, cot, cot_other, gain)


def ffn_weights_kernel(h2_ref, cot_ref, cot_other_ref, d_gate_ref, d_up_ref, act_ref, out_ref):
    for k in range(4):
        columns = slice(k * 256, (k + 1) * 256)
        h2 = h2_ref[:, columns]
        cot = jnp.concatenate([cot_ref[:, columns], cot_other_ref[:, columns]], axis=0)
        for n, (left, right) in enumerate(((h2, d_gate_ref), (h2, d_up_ref), (cot, act_ref))):
            block = dot(left, right[...], ((0,), (0,))).astype(BF16)
            for i in range(4):
                out_ref[4 * k + i, n] = block[i * 64 : (i + 1) * 64]


def ffn_weights(h2, cot, cot_other, d_gate, d_up, act):
    return pl.pallas_call(
        ffn_weights_kernel,
        in_specs=[VMEM] * 6,
        out_specs=VMEM,
        out_shape=jax.ShapeDtypeStruct((16, 3, 64, FSL), BF16),
        compiler_params=pltpu.CompilerParams(vmem_limit_bytes=40 * 2**20),
        cost_estimate=pl.CostEstimate(flops=4 * 10**9, bytes_accessed=11 * 10**6, transcendentals=0),
    )(h2, cot, cot_other, d_gate, d_up, act)


def assemble_ffn_kernel(in_ref, gate_ref, up_ref, down_ref):
    for a in range(2):
        rows = pl.ds(a * 64, 64)
        gate_ref[rows, :] = jnp.concatenate([in_ref[a, 0, 0], in_ref[a, 1, 0]], axis=1).astype(F32)
        up_ref[rows, :] = jnp.concatenate([in_ref[a, 0, 1], in_ref[a, 1, 1]], axis=1).astype(F32)
    for i in range(2):
        block = jnp.concatenate([in_ref[0, i, 2], in_ref[1, i, 2]], axis=0).astype(F32)
        block = jnp.concatenate([block, jnp.zeros((128, 64), F32)], axis=1)
        down_ref[:, i * 128 : (i + 1) * 128] = block.T[:FSL]


def assemble_ffn(gathered):
    return pl.pallas_call(
        assemble_ffn_kernel,
        grid=(4,),
        in_specs=[pl.BlockSpec((2, 2, 3, 64, FSL), lambda i: (0, i, 0, 0, 0))],
        out_specs=(
            pl.BlockSpec((TOK, 2 * FSL), lambda i: (0, i)),
            pl.BlockSpec((TOK, 2 * FSL), lambda i: (0, i)),
            pl.BlockSpec((FSL, 256), lambda i: (0, i)),
        ),
        out_shape=(
            jax.ShapeDtypeStruct((TOK, FF), F32),
            jax.ShapeDtypeStruct((TOK, FF), F32),
            jax.ShapeDtypeStruct((FSL, D), F32),
        ),
        compiler_params=pltpu.CompilerParams(vmem_limit_bytes=32 * 2**20),
        cost_estimate=pl.CostEstimate(flops=0, bytes_accessed=11 * 10**6, transcendentals=0),
    )(gathered)


def assemble_attention_kernel(
    core_ref, same_ref, other_ref, query_ref, key_ref, value_ref, out_ref, gain_ref, stack
):
    core = core_ref[0]
    stack[core] = same_ref[...]
    stack[1 - core] = other_ref[...]
    for z in range(4):
        for c in range(2):
            m = 2 * z + c
            both = jnp.concatenate([stack[c, z, :64], stack[c, 4 + z, :64]], axis=0).astype(F32)
            query_ref[:, m * 128 : (m + 1) * 128] = both[:, :128]
            out_ref[:, m * 128 : (m + 1) * 128] = both[:, 256:].T
        for lo, ref in ((128, key_ref), (192, value_ref)):
            for a in range(2):
                ref[a * 64 : (a + 1) * 64, z * 128 : (z + 1) * 128] = jnp.concatenate(
                    [stack[c, 4 * a + z, :64, lo : lo + 64] for c in range(2)], axis=1
                ).astype(F32)
    for a in range(2):
        gain_ref[a] = sum(stack[c, 4 * a + z, 64:].astype(F32) for c in range(2) for z in range(4))


def assemble_attention(core, same, other):
    outs = pl.pallas_call(
        assemble_attention_kernel,
        out_shape=(
            jax.ShapeDtypeStruct((TOK, D), F32),
            jax.ShapeDtypeStruct((TOK, KVH * HD), F32),
            jax.ShapeDtypeStruct((TOK, KVH * HD), F32),
            jax.ShapeDtypeStruct((TOK, D), F32),
            jax.ShapeDtypeStruct((2, 16, 384), F32),
        ),
        in_specs=[SMEM, VMEM, VMEM],
        out_specs=(VMEM,) * 5,
        scratch_shapes=[pltpu.VMEM((2, 8, 80, 384), BF16)],
        compiler_params=pltpu.CompilerParams(vmem_limit_bytes=32 * 2**20),
        cost_estimate=pl.CostEstimate(flops=0, bytes_accessed=3 * 10**6, transcendentals=0),
    )(core, same, other)
    return outs[:4] + (outs[4][:, 0, :],)


def rotate(values, cosine, sine):
    half = HD // 2
    turned = jnp.concatenate([-values[:, half:], values[:, :half]], axis=1)
    return values * cosine + turned * sine


def unrotate(grads, cosine, sine):
    half = HD // 2
    scaled = grads * sine
    turned = jnp.concatenate([scaled[:, half:], -scaled[:, :half]], axis=1)
    return grads * cosine + turned


def whole(shape):
    return pl.BlockSpec(shape, lambda i: (0,) * len(shape))


def half_rows(columns):
    return (
        pl.BlockSpec((256, columns), lambda i: (jnp.minimum(i, 1), 0)),
        pl.BlockSpec((256, columns), lambda i: (jnp.maximum(i - 2, 0), 0)),
    )


def token_rows(columns):
    return pl.BlockSpec((256, columns), lambda i: (i, 0))


def project_kernel(
    x_ref, x_other_ref, weights_ref, gain_ref, gain_query_ref, gain_key_ref, cos_ref, sin_ref,
    proj_ref, query_ref, kv_ref, w_qkv,
):
    i = pl.program_id(0)

    @pl.when(i == 0)
    def _():
        for k in range(8):
            w_qkv[k * 128 : (k + 1) * 128, :] = weights_ref[k, :128, :]

    x = jnp.where(i < 2, x_ref[...], x_other_ref[...]).astype(F32)
    h1 = (x * inv_rms(x) * gain_ref[...]).astype(BF16)
    proj = dot(h1, w_qkv[...])
    proj_ref[...] = proj
    turned = []
    for h, gain in ((0, gain_query_ref), (1, gain_query_ref), (2, gain_key_ref)):
        part = proj[:, h * HD : (h + 1) * HD]
        turned.append(rotate(part * inv_rms(part) * gain[...], cos_ref[...], sin_ref[...]).astype(BF16))
    query_ref[0] = turned[0] * jnp.asarray(HD ** -0.5, BF16)
    query_ref[1] = turned[1] * jnp.asarray(HD ** -0.5, BF16)
    kv_ref[...] = jnp.concatenate([turned[2], proj[:, 3 * HD :].astype(BF16)], axis=1)


def project(x, x_other, weights, gain, gain_query, gain_key, cosine, sine):
    first, last = half_rows(D)
    return pl.pallas_call(
        project_kernel,
        grid=(4,),
        in_specs=[
            first, last, whole((8, 144, 256)), whole((1, D)), whole((1, HD)), whole((1, HD)),
            token_rows(HD), token_rows(HD),
        ],
        out_specs=(token_rows(256), pl.BlockSpec((2, 256, HD), lambda i: (0, i, 0)), token_rows(2 * HD)),
        out_shape=(
            jax.ShapeDtypeStruct((HALF, 256), F32),
            jax.ShapeDtypeStruct((2, HALF, HD), BF16),
            jax.ShapeDtypeStruct((HALF, 2 * HD), BF16),
        ),
        scratch_shapes=[pltpu.VMEM((D, 256), BF16)],
        compiler_params=pltpu.CompilerParams(vmem_limit_bytes=32 * 2**20),
        cost_estimate=pl.CostEstimate(flops=5 * 10**8, bytes_accessed=4 * 10**6, transcendentals=0),
    )(x, x_other, weights, gain, gain_query, gain_key, cosine, sine)


def project_back_kernel(
    x_ref, x_other_ref, weights_ref, gain_ref, gain_query_ref, gain_key_ref, cos_ref, sin_ref,
    proj_ref, dq_ref, dkv_ref, dkv_peer_ref,
    mine_ref, low_ref, weight_ref, gain_grad_ref, query_grad_ref, key_grad_ref, w_qkv, total,
):
    i = pl.program_id(0)

    @pl.when(i == 0)
    def _():
        for k in range(8):
            w_qkv[k * 128 : (k + 1) * 128, :] = weights_ref[k, :128, :]
        total[...] = jnp.zeros_like(total)
        for ref in (gain_grad_ref, query_grad_ref, key_grad_ref):
            ref[...] = jnp.zeros_like(ref)

    dkv = (dkv_ref[...] + dkv_peer_ref[...].astype(F32)).astype(BF16)
    grads = (dq_ref[0], dq_ref[1], dkv[:, :HD])
    outs = []
    for h, gain, grad_ref in (
        (0, gain_query_ref, query_grad_ref),
        (1, gain_query_ref, query_grad_ref),
        (2, gain_key_ref, key_grad_ref),
    ):
        part = proj_ref[:, h * HD : (h + 1) * HD]
        scale = inv_rms(part)
        normed = part * scale
        grad = unrotate(grads[h].astype(F32), cos_ref[...], sin_ref[...])
        grad_ref[...] += jnp.sum(grad * normed, axis=0, keepdims=True)
        outs.append(norm_back(grad * gain[...], normed, scale).astype(BF16))
    dqkv = jnp.concatenate(outs + [dkv[:, HD:]], axis=1)
    x = jnp.where(i < 2, x_ref[...], x_other_ref[...]).astype(F32)
    n1 = x * inv_rms(x)
    h1 = (n1 * gain_ref[...]).astype(BF16)
    dh1 = dot(dqkv, w_qkv[...], ((1,), (1,)))
    gain_grad_ref[...] += jnp.sum(dh1 * n1, axis=0, keepdims=True)
    total[...] += dot(h1, dqkv, ((0,), (0,)))

    @pl.when(i < 2)
    def _():
        mine_ref[...] = dh1

    @pl.when(i >= 2)
    def _():
        low_ref[...] = dh1.astype(BF16)

    @pl.when(i == 3)
    def _():
        weight_ref[...] = total[...].astype(BF16)


def project_back(x, x_other, weights, gain, gain_query, gain_key, cosine, sine, proj, dq, dkv, dkv_peer):
    first, last = half_rows(D)
    return pl.pallas_call(
        project_back_kernel,
        grid=(4,),
        in_specs=[
            first, last, whole((8, 144, 256)), whole((1, D)), whole((1, HD)), whole((1, HD)),
            token_rows(HD), token_rows(HD), token_rows(256),
            pl.BlockSpec((2, 256, HD), lambda i: (0, i, 0)), token_rows(2 * HD), token_rows(2 * HD),
        ],
        out_specs=(first, last, whole((D, 256)), whole((1, D)), whole((1, HD)), whole((1, HD))),
        out_shape=(
            jax.ShapeDtypeStruct((512, D), F32),
            jax.ShapeDtypeStruct((512, D), BF16),
            jax.ShapeDtypeStruct((D, 256), BF16),
            jax.ShapeDtypeStruct((1, D), F32),
            jax.ShapeDtypeStruct((1, HD), F32),
            jax.ShapeDtypeStruct((1, HD), F32),
        ),
        scratch_shapes=[pltpu.VMEM((D, 256), BF16), pltpu.VMEM((D, 256), F32)],
        compiler_params=pltpu.CompilerParams(vmem_limit_bytes=32 * 2**20),
        cost_estimate=pl.CostEstimate(flops=10**9, bytes_accessed=6 * 10**6, transcendentals=0),
    )(x, x_other, weights, gain, gain_query, gain_key, cosine, sine, proj, dq, dkv, dkv_peer)


def inv_rms(values):
    return lax.rsqrt(jnp.mean(values * values, axis=-1, keepdims=True) + EPS)


def norm_back(grads, normed, scale):
    return scale * (grads - normed * jnp.mean(grads * normed, axis=-1, keepdims=True))


def per_device(
    tokens, cotangent, places, doc_split,
    w_query, w_key, w_value, w_out, w_gate, w_up, w_down,
    norm_attn, norm_ffn, norm_query, norm_key,
):
    a, z, c = lax.axis_index("a"), lax.axis_index("z"), lax.axis_index("c")
    m = z * 2 + c
    own_tokens, own_cot = tokens[0], cotangent[0]

    gains = jnp.concatenate([norm_attn, norm_ffn, norm_query, norm_key, jnp.zeros((240,), BF16)])
    gains = jnp.concatenate([gains.reshape(2, 256), jnp.zeros((14, 256), BF16)], axis=0)
    qkv_own = jnp.concatenate(
        [
            lax.dynamic_slice_in_dim(w_query, m * 128, 128, 1),
            lax.dynamic_slice_in_dim(w_key, m * 64, 64, 1),
            lax.dynamic_slice_in_dim(w_value, m * 64, 64, 1),
        ],
        axis=1,
    )
    qkv_own = jnp.concatenate([qkv_own, gains], axis=0)
    qkv_all = lax.all_to_all(
        jnp.broadcast_to(qkv_own[None], (8, 144, 256)), FS, split_axis=0, concat_axis=0, tiled=True
    )
    w_down_m = fetch_shard(w_down)
    x_same = ring(own_tokens)
    x_other = swap(x_same, "c")
    gain_parts = qkv_all[:, 128:130].reshape(8, 512).astype(F32)
    gain_attn = gain_parts[:, :128].reshape(D)
    gain_ffn = gain_parts[:, 128:256].reshape(D)
    gain_query = gain_parts[:, 256:264].reshape(HD)
    gain_key = gain_parts[:, 264:272].reshape(HD)

    wide_own = jnp.concatenate(
        [
            w_out,
            lax.dynamic_slice_in_dim(w_gate, m * FSL, FSL, 1),
            jnp.zeros((TOK, 64), BF16),
            lax.dynamic_slice_in_dim(w_up, m * FSL, FSL, 1),
        ],
        axis=1,
    )
    wide = lax.all_gather(wide_own, FS, axis=0)

    block_of = places[0].reshape(32, BLK)[:, 0] // BLK
    wanted = []
    for half in (a, 1 - a):
        for dc in range(2):
            for dz in range(4):
                device = half * 8 + ((z - dz) % 4) * 2 + (c ^ dc)
                wanted += [device * 2, device * 2 + 1]
    wanted = jnp.stack(wanted)
    blocks = jnp.sum(
        jnp.where(wanted[:, None] == jnp.arange(32)[None, :], block_of[None, :], 0), axis=1
    ).astype(jnp.int32)
    place = (blocks[:16, None] * BLK + jnp.arange(BLK)[None, :]).reshape(HALF)
    split = doc_split[0]
    position = (place - jnp.where(place >= split, split, 0)).astype(F32)
    inv_freq = THETA ** (-2.0 * jnp.arange(HD // 2).astype(F32) / HD)
    phases = position[:, None] * inv_freq[None, :]
    phases = jnp.concatenate([phases, phases], axis=-1)
    cosine, sine = jnp.cos(phases), jnp.sin(phases)

    tables = (gain_attn[None], gain_query[None], gain_key[None], cosine, sine)
    proj, q_scaled, kv_own = project(x_same, x_other, qkv_all, *tables)
    kv_peer = swap(kv_own, "a")
    cot_same = ring(after(own_cot, kv_own))
    attended, sums = attention_forward(blocks, doc_split, q_scaled, kv_own, kv_peer)

    heads_same = heads_ring(attended)
    heads_same, cot_same, w_down_m = after((heads_same, cot_same, w_down_m))
    heads_other = swap(heads_same, "c")
    cot_other = swap(cot_same, "c")
    order = jnp.stack(
        [((z - dz) % 4) * 2 + (c ^ dc) for dc in range(2) for dz in range(4)]
    ).astype(jnp.int32)
    h2, d_gate, d_up, act, dh2_mine, dh2_low, out_mine, out_low, own_y1, grad_gain_ffn = ffn(
        order, x_same, x_other, heads_same, heads_other, wide, w_down_m, cot_same, cot_other, gain_ffn[None]
    )

    dh2_same = add_cores(dh2_mine, dh2_low)
    ffn_terms = ffn_weights(h2, cot_same, cot_other, d_gate, d_up, act)
    ffn_got = lax.all_to_all(ffn_terms, ("y", "b", "a"), split_axis=0, concat_axis=0, tiled=True)
    dh2 = add_ring(dh2_same, ffn_terms)
    own_r2 = inv_rms(own_y1)
    own_n2 = own_y1 * own_r2
    dy1 = own_cot.astype(F32) + norm_back(dh2 * gain_ffn, own_n2, own_r2)
    dz_low = dy1.astype(BF16)
    dz_same = ring(dz_low)
    dz_other = swap(dz_same, "c")
    out_same = add_cores(out_mine, after(out_low, dz_same))

    w_out_m = lax.dynamic_index_in_dim(wide, m, 0, keepdims=False)[:, :D]
    d_att = jnp.concatenate(
        [dot(part, w_out_m, ((1,), (1,))).astype(BF16) for part in (dz_same, dz_other)], axis=0
    )
    dq_rot, dkv_own, dkv_peer = attention_backward(
        blocks, doc_split, q_scaled, kv_own, kv_peer, attended, d_att, sums
    )
    layer_out = (own_y1 + add_ring(out_same)).astype(BF16)
    dkv_peer = swap(dkv_peer, "a")
    ffn_piece = jnp.sum(after(ffn_got, dq_rot).astype(F32), axis=0).astype(BF16)
    ffn_piece = jnp.concatenate([ffn_piece[:2], cross(ffn_piece[2])[None]], axis=0)
    dkv_peer, ffn_piece = after((dkv_peer, ffn_piece))
    ffn_all = lax.all_gather(ffn_piece, CTX, axis=0).reshape(2, 8, 3, 64, FSL)
    out_terms = dot(dz_same, attended[:512], ((0,), (0,))) + dot(dz_other, attended[512:], ((0,), (0,)))
    dh1_mine, dh1_low, qkv_terms, grad_gain_attn, grad_gain_query, grad_gain_key = project_back(
        x_same, x_other, qkv_all, *tables, proj, dq_rot, dkv_own, dkv_peer
    )

    attn_terms = jnp.concatenate([qkv_terms, out_terms.astype(BF16)], axis=1)
    gain_terms = jnp.concatenate(
        [
            grad_gain_attn.reshape(8, 128),
            grad_gain_ffn.reshape(8, 128),
            grad_gain_query.reshape(8, 8),
            grad_gain_key.reshape(8, 8),
        ],
        axis=1,
    ).reshape(8, 2, 1, 136)
    gain_terms = jnp.pad(gain_terms, ((0, 0), (0, 0), (0, 15), (0, 384 - 136)))
    terms = jnp.concatenate([attn_terms.reshape(8, 2, 64, 384), gain_terms.astype(BF16)], axis=2)
    terms = terms.reshape(16, 80, 384)
    dh1_same = add_cores(dh1_mine, dh1_low, terms)
    dh1 = add_ring(dh1_same)
    own_x = own_tokens.astype(F32)
    own_r1 = inv_rms(own_x)
    grad_tokens = (dy1 + norm_back(dh1 * gain_attn, own_x * own_r1, own_r1)).astype(BF16)
    got = lax.all_to_all(terms, ("y", "b", "a"), split_axis=0, concat_axis=0, tiled=True)
    piece = jnp.sum(after(got, dh1_same).astype(F32), axis=0).astype(BF16)
    piece = jnp.concatenate([piece[:, :256], cross(piece[:, 256:])], axis=1)
    piece, grad_tokens = after((piece, grad_tokens))
    ffn_grads = assemble_ffn(ffn_all)
    piece, ffn_grads, layer_out = after((piece, ffn_grads, layer_out))
    grad_gate, grad_up, grad_down = ffn_grads
    same = lax.all_to_all(
        jnp.broadcast_to(piece[None], (8, 80, 384)), ("a", "z"), split_axis=0, concat_axis=0, tiled=True
    )
    first_core = jnp.full((1,), c, jnp.int32)
    grad_query, grad_key, grad_value, grad_out, gain_sum = assemble_attention(
        first_core, same, swap(same, "c")
    )
    gain_sum = gain_sum[:, :136].reshape(272)
    return (
        layer_out[None],
        grad_tokens[None],
        grad_query,
        grad_key,
        grad_value,
        grad_out,
        grad_gate,
        grad_up,
        grad_down,
        gain_sum[:128],
        gain_sum[128:256],
        gain_sum[256:264],
        gain_sum[264:],
    )


def solution(mesh):
    fine = Mesh(mesh.devices.reshape(NA, NZ, NC, NY, NB), CTX + FS)
    rows = P(FS, CTX, None)
    shard = P(FS, None)
    in_specs = (rows, rows, shard, P(FS)) + (shard,) * 7 + (P(FS),) * 4
    out_specs = (rows, rows) + (shard,) * 7 + (P(FS),) * 4
    return jax.shard_map(
        per_device, mesh=fine, in_specs=in_specs, out_specs=out_specs, check_vma=False
    )
```

```python
import functools

import jax
import jax.numpy as jnp
import numpy as np
from jax import lax
from jax.experimental import pallas as pl
from jax.experimental.pallas import tpu as pltpu
from jax.sharding import Mesh
from jax.sharding import PartitionSpec as P

D = 1024
H = 16
KVH = 8
HD = 64
FF = 4608
TOK = 128
LEN = 2048
HALF = 1024
FSL = FF // 8
BLK = 64
EPS = 1e-05
THETA = 1000000.0
F32 = jnp.float32
BF16 = jnp.bfloat16
NA, NZ, NC, NY, NB = 2, 4, 2, 4, 2
CTX = ("a", "z", "c")
FS = ("y", "b")


def dot(left, right, dims=((1,), (0,))):
    return lax.dot_general(left, right, (dims, ((), ())), preferred_element_type=F32)


def shift(value, axis, size, step):
    return lax.ppermute(value, axis, [(i, (i + step) % size) for i in range(size)])


def swap(value, axis):
    return shift(value, axis, 2, 1)


def after(value, *earlier):
    return lax.optimization_barrier((value, earlier))[0]


def ring(own):
    return jnp.concatenate([own] + [shift(own, "z", NZ, step) for step in (1, 2, 3)], axis=0)


def both_cores(same):
    return jnp.concatenate([same, swap(same, "c")], axis=0)


def add_cores(mine, low, *earlier):
    return mine + after(swap(low, "c"), *earlier).astype(F32)


def add_ring(mine, *earlier):
    low = mine.astype(BF16)
    parts = [shift(low[step * TOK : (step + 1) * TOK], "z", NZ, -step) for step in (1, 2, 3)]
    if earlier:
        parts = after(parts, *earlier)
    total = mine[:TOK]
    for part in parts:
        total = total + part.astype(F32)
    return total


def heads_ring(own):
    return jnp.stack([own] + [shift(own, "z", NZ, step) for step in (1, 2, 3)])


def cross(value):
    pairs = [(m * 8 + j, j * 8 + m) for m in range(8) for j in range(8)]
    return lax.ppermute(value, ("z", "c", "y", "b"), pairs)


def fetch_shard(value):
    pairs = []
    for z, c, y, b in np.ndindex(NZ, NC, NY, NB):
        source = (((y + z) % 4 * 2 + b) * 4 + z) * 2 + c
        pairs.append((source, ((z * 2 + c) * 4 + y) * 2 + b))
    return lax.ppermute(value, ("z", "c", "y", "b"), pairs)


KC = 512


def sort_keys(kb_ref, own_ref, peer_ref, keys, values, values_one):
    for i in range(32):
        src = own_ref if i < 16 else peer_ref
        r = (i % 16) * BLK
        rows = pl.ds(pl.multiple_of(kb_ref[i] * BLK, BLK), BLK)
        block = src[r : r + BLK, :]
        keys[rows, :] = block[:, :HD]
        part = block[:, HD:]
        if values is not None:
            values[rows, :] = part
        if values_one is not None:
            values_one[rows, :] = jnp.concatenate([part, jnp.ones_like(part)], axis=1)


def key_range(p, split):
    first = jnp.where(p * BLK >= split, split // KC, 0)
    return first, (p * BLK) // KC + 1


def attention_forward_kernel(kb_ref, split_ref, q_ref, own_ref, peer_ref, out_ref, sum_ref, keys, values_one):
    sort_keys(kb_ref, own_ref, peer_ref, keys, None, values_one)
    split = split_ref[0]

    def one_block(i, _):
        p = kb_ref[i]
        rows = pl.ds(pl.multiple_of(i * BLK, BLK), BLK)
        q = jnp.concatenate([q_ref[0, rows, :], q_ref[1, rows, :]], axis=0)
        row_place = p * BLK + lax.rem(lax.broadcasted_iota(jnp.int32, (2 * BLK, KC), 0), BLK)
        start = jnp.where(row_place >= split, split, 0)
        col = lax.broadcasted_iota(jnp.int32, (2 * BLK, KC), 1)

        def one_chunk(ck, acc):
            at = pl.multiple_of(ck * KC, KC)
            s = dot(q, keys[pl.ds(at, KC), :], ((1,), (1,)))
            key_place = col + at
            seen = (key_place <= row_place) & (key_place >= start)
            e = jnp.where(seen, jnp.exp(s), 0.0).astype(BF16)
            return acc + dot(e, values_one[pl.ds(at, KC), :])

        lo, hi = key_range(p, split)
        acc = lax.fori_loop(lo, hi, one_chunk, jnp.zeros((2 * BLK, 2 * HD), F32))
        o = acc[:, :HD] / acc[:, HD:]
        out_ref[rows, :] = jnp.concatenate([o[:BLK], o[BLK:]], axis=1).astype(BF16)
        sum_ref[pl.ds(pl.multiple_of(i * 8, 8), 8), :] = acc.T[HD : HD + 8, :]
        return 0

    lax.fori_loop(0, 16, one_block, 0)


SMEM = pl.BlockSpec(memory_space=pltpu.SMEM)
VMEM = pl.BlockSpec(memory_space=pltpu.VMEM)


def attention_forward(blocks, split, queries, own, peer):
    return pl.pallas_call(
        attention_forward_kernel,
        out_shape=(
            jax.ShapeDtypeStruct((HALF, 2 * HD), BF16),
            jax.ShapeDtypeStruct((128, 128), F32),
        ),
        in_specs=[SMEM, SMEM, VMEM, VMEM, VMEM],
        out_specs=(VMEM, VMEM),
        scratch_shapes=[pltpu.VMEM((LEN, HD), BF16), pltpu.VMEM((LEN, 2 * HD), BF16)],
        compiler_params=pltpu.CompilerParams(vmem_limit_bytes=32 * 2**20),
        cost_estimate=pl.CostEstimate(flops=5 * 10**8, bytes_accessed=2 * 10**6, transcendentals=0),
    )(blocks, split, queries, own, peer)


def attention_backward_kernel(
    kb_ref, split_ref, q_ref, own_ref, peer_ref, att_ref, do_ref, sum_ref,
    dq_ref, down_ref, dpeer_ref, keys, values, keys_t, dk, dv,
):
    sort_keys(kb_ref, own_ref, peer_ref, keys, values, None)
    for i in range(LEN // KC):
        keys_t[:, i * KC : (i + 1) * KC] = keys[i * KC : (i + 1) * KC, :].T
    dk[...] = jnp.zeros_like(dk)
    dv[...] = jnp.zeros_like(dv)
    split = split_ref[0]

    def one_block(i, _):
        p = kb_ref[i]
        rows = pl.ds(pl.multiple_of(i * BLK, BLK), BLK)
        q = jnp.concatenate([q_ref[0, rows, :], q_ref[1, rows, :]], axis=0)
        pair = do_ref[rows, :]
        do = jnp.concatenate([pair[:, :HD], pair[:, HD:]], axis=0)
        prod = pair.astype(F32) * att_ref[rows, :].astype(F32)
        prod = jnp.concatenate([prod[:, :HD], prod[:, HD:]], axis=0)
        inner = jnp.sum(prod.T, axis=0, keepdims=True)
        inv = 1.0 / sum_ref[pl.ds(pl.multiple_of(i * 8, 8), 8), :][:1]
        row_place = p * BLK + lax.rem(lax.broadcasted_iota(jnp.int32, (KC, 2 * BLK), 1), BLK)
        start = jnp.where(row_place >= split, split, 0)
        col = lax.broadcasted_iota(jnp.int32, (KC, 2 * BLK), 0)

        def one_chunk(ck, dqt):
            at = pl.multiple_of(ck * KC, KC)
            here = pl.ds(at, KC)
            s = dot(keys[here, :], q, ((1,), (1,)))
            dp = dot(values[here, :], do, ((1,), (1,)))
            key_place = col + at
            seen = (key_place <= row_place) & (key_place >= start)
            prob = jnp.where(seen, jnp.exp(s), 0.0) * inv
            ds = (prob * (dp - inner)).astype(BF16)
            dv[here, :] += dot(prob.astype(BF16), do)
            dk[here, :] += dot(ds, q)
            return dqt + dot(keys_t[:, here], ds)

        lo, hi = key_range(p, split)
        dqt = lax.fori_loop(lo, hi, one_chunk, jnp.zeros((HD, 2 * BLK), F32))
        dq = (dqt.T * (HD ** -0.5)).astype(BF16)
        dq_ref[0, rows, :] = dq[:BLK]
        dq_ref[1, rows, :] = dq[BLK:]
        return 0

    lax.fori_loop(0, 16, one_block, 0)
    for i in range(32):
        rows = pl.ds(pl.multiple_of(kb_ref[i] * BLK, BLK), BLK)
        both = jnp.concatenate([dk[rows, :], dv[rows, :]], axis=1)
        r = (i % 16) * BLK
        if i < 16:
            down_ref[r : r + BLK, :] = both
        else:
            dpeer_ref[r : r + BLK, :] = both.astype(BF16)


def attention_backward(blocks, split, queries, own, peer, attended, grad, sums):
    return pl.pallas_call(
        attention_backward_kernel,
        out_shape=(
            jax.ShapeDtypeStruct((2, HALF, HD), BF16),
            jax.ShapeDtypeStruct((HALF, 2 * HD), F32),
            jax.ShapeDtypeStruct((HALF, 2 * HD), BF16),
        ),
        in_specs=[SMEM, SMEM] + [VMEM] * 6,
        out_specs=(VMEM, VMEM, VMEM),
        scratch_shapes=[
            pltpu.VMEM((LEN, HD), BF16),
            pltpu.VMEM((LEN, HD), BF16),
            pltpu.VMEM((HD, LEN), BF16),
            pltpu.VMEM((LEN, HD), F32),
            pltpu.VMEM((LEN, HD), F32),
        ],
        compiler_params=pltpu.CompilerParams(vmem_limit_bytes=32 * 2**20),
        cost_estimate=pl.CostEstimate(flops=5 * 10**8, bytes_accessed=4 * 10**6, transcendentals=0),
    )(blocks, split, queries, own, peer, attended, grad, sums)


def ffn_kernel(
    order_ref, x_ref, x_other_ref, same_ref, other_ref, weights_ref, down_ref, cot_ref, cot_other_ref, gain_ref,
    h2_ref, d_gate_ref, d_up_ref, act_ref, dh2_mine_ref, dh2_low_ref, out_mine_ref, out_low_ref,
    y1_ref, gain_grad_ref, w_out, w_gate, w_up,
):
    i = pl.program_id(0)

    @pl.when(i == 0)
    def _():
        for k in range(8):
            rows = slice(k * 128, (k + 1) * 128)
            w_out[rows, :] = weights_ref[order_ref[k], :, :D]
            w_gate[rows, :] = weights_ref[k, :, D : D + FSL]
            w_up[rows, :] = weights_ref[k, :, D + 640 : D + 640 + FSL]
        gain_grad_ref[...] = jnp.zeros_like(gain_grad_ref)

    chunks = []
    for half in range(2):
        dc, dz = i // 2, (i % 2) * 2 + half
        parts = []
        for ref, core in ((same_ref, dc), (other_ref, 1 - dc)):
            for step in range(4):
                row = (core * 4 + (dz - step + 4) % 4) * TOK
                parts.append(ref[step, pl.ds(pl.multiple_of(row, TOK), TOK), :])
        chunks.append(jnp.concatenate(parts, axis=1))
    att = jnp.concatenate(chunks, axis=0)
    x = jnp.where(i < 2, x_ref[...], x_other_ref[...]).astype(F32)
    y1 = x + dot(att, w_out[...])
    r2 = lax.rsqrt(jnp.mean(y1 * y1, axis=1, keepdims=True) + EPS)
    n2 = y1 * r2
    h2 = (n2 * gain_ref[...]).astype(BF16)
    h2_ref[...] = h2

    @pl.when(i == 0)
    def _():
        y1_ref[...] = y1[:TOK]

    gate = dot(h2, w_gate[...])
    up = dot(h2, w_up[...])
    cot = jnp.where(i < 2, cot_ref[...], cot_other_ref[...])
    da = dot(cot, down_ref[...], ((1,), (1,)))
    sg = 1.0 / (1.0 + jnp.exp(-gate))
    silu = gate * sg
    act = (silu * up).astype(BF16)
    d_up = (da * silu).astype(BF16)
    d_gate = (da * up * (sg * (1.0 + gate * (1.0 - sg)))).astype(BF16)
    act_ref[...] = act
    d_up_ref[...] = d_up
    d_gate_ref[...] = d_gate
    dh2 = dot(d_gate, w_gate[...], ((1,), (1,))) + dot(d_up, w_up[...], ((1,), (1,)))
    gain_grad_ref[...] += jnp.sum(dh2 * n2, axis=0, keepdims=True)
    out = dot(act, down_ref[...])

    @pl.when(i < 2)
    def _():
        dh2_mine_ref[...] = dh2
        out_mine_ref[...] = out

    @pl.when(i >= 2)
    def _():
        dh2_low_ref[...] = dh2.astype(BF16)
        out_low_ref[...] = out.astype(BF16)


def ffn(order, x, x_other, same, other, weights, down, cot, cot_other, gain):
    rows = 256

    tokens = pl.BlockSpec((rows, D), lambda i: (i, 0))
    hidden = pl.BlockSpec((rows, FSL), lambda i: (i, 0))
    first = pl.BlockSpec((rows, D), lambda i: (jnp.minimum(i, 1), 0))
    last = pl.BlockSpec((rows, D), lambda i: (jnp.maximum(i - 2, 0), 0))
    return pl.pallas_call(
        ffn_kernel,
        grid=(HALF // rows,),
        in_specs=[
            SMEM, first, last, whole((4, HALF, 128)), whole((4, HALF, 128)),
            whole((8, 128, 2240)), whole((FSL, D)), first, last, whole((1, D)),
        ],
        out_specs=(tokens, hidden, hidden, hidden, first, last, first, last, whole((TOK, D)), whole((1, D))),
        out_shape=(
            jax.ShapeDtypeStruct((HALF, D), BF16),
            jax.ShapeDtypeStruct((HALF, FSL), BF16),
            jax.ShapeDtypeStruct((HALF, FSL), BF16),
            jax.ShapeDtypeStruct((HALF, FSL), BF16),
            jax.ShapeDtypeStruct((512, D), F32),
            jax.ShapeDtypeStruct((512, D), BF16),
            jax.ShapeDtypeStruct((512, D), F32),
            jax.ShapeDtypeStruct((512, D), BF16),
            jax.ShapeDtypeStruct((TOK, D), F32),
            jax.ShapeDtypeStruct((1, D), F32),
        ),
        scratch_shapes=[
            pltpu.VMEM((D, D), BF16),
            pltpu.VMEM((D, FSL), BF16),
            pltpu.VMEM((D, FSL), BF16),
        ],
        compiler_params=pltpu.CompilerParams(vmem_limit_bytes=48 * 2**20),
        cost_estimate=pl.CostEstimate(flops=11 * 10**9, bytes_accessed=24 * 10**6, transcendentals=10**6),
    )(order, x, x_other, same, other, weights, down, cot, cot_other, gain)


def ffn_weights_kernel(h2_ref, cot_ref, cot_other_ref, d_gate_ref, d_up_ref, act_ref, out_ref):
    for k in range(4):
        columns = slice(k * 256, (k + 1) * 256)
        h2 = h2_ref[:, columns]
        cot = jnp.concatenate([cot_ref[:, columns], cot_other_ref[:, columns]], axis=0)
        for n, (left, right) in enumerate(((h2, d_gate_ref), (h2, d_up_ref), (cot, act_ref))):
            block = dot(left, right[...], ((0,), (0,))).astype(BF16)
            for i in range(4):
                out_ref[4 * k + i, n] = block[i * 64 : (i + 1) * 64]


def ffn_weights(h2, cot, cot_other, d_gate, d_up, act):
    return pl.pallas_call(
        ffn_weights_kernel,
        in_specs=[VMEM] * 6,
        out_specs=VMEM,
        out_shape=jax.ShapeDtypeStruct((16, 3, 64, FSL), BF16),
        compiler_params=pltpu.CompilerParams(vmem_limit_bytes=40 * 2**20),
        cost_estimate=pl.CostEstimate(flops=4 * 10**9, bytes_accessed=11 * 10**6, transcendentals=0),
    )(h2, cot, cot_other, d_gate, d_up, act)


def assemble_ffn_kernel(in_ref, gate_ref, up_ref, down_ref):
    for a in range(2):
        rows = pl.ds(a * 64, 64)
        gate_ref[rows, :] = jnp.concatenate([in_ref[a, 0, 0], in_ref[a, 1, 0]], axis=1).astype(F32)
        up_ref[rows, :] = jnp.concatenate([in_ref[a, 0, 1], in_ref[a, 1, 1]], axis=1).astype(F32)
    for i in range(2):
        block = jnp.concatenate([in_ref[0, i, 2], in_ref[1, i, 2]], axis=0).astype(F32)
        block = jnp.concatenate([block, jnp.zeros((128, 64), F32)], axis=1)
        down_ref[:, i * 128 : (i + 1) * 128] = block.T[:FSL]


def assemble_ffn(gathered):
    return pl.pallas_call(
        assemble_ffn_kernel,
        grid=(4,),
        in_specs=[pl.BlockSpec((2, 2, 3, 64, FSL), lambda i: (0, i, 0, 0, 0))],
        out_specs=(
            pl.BlockSpec((TOK, 2 * FSL), lambda i: (0, i)),
            pl.BlockSpec((TOK, 2 * FSL), lambda i: (0, i)),
            pl.BlockSpec((FSL, 256), lambda i: (0, i)),
        ),
        out_shape=(
            jax.ShapeDtypeStruct((TOK, FF), F32),
            jax.ShapeDtypeStruct((TOK, FF), F32),
            jax.ShapeDtypeStruct((FSL, D), F32),
        ),
        compiler_params=pltpu.CompilerParams(vmem_limit_bytes=32 * 2**20),
        cost_estimate=pl.CostEstimate(flops=0, bytes_accessed=11 * 10**6, transcendentals=0),
    )(gathered)


def assemble_attention_kernel(
    core_ref, same_ref, other_ref, query_ref, key_ref, value_ref, out_ref, gain_ref, stack
):
    core = core_ref[0]
    stack[core] = same_ref[...]
    stack[1 - core] = other_ref[...]
    for z in range(4):
        for c in range(2):
            m = 2 * z + c
            both = jnp.concatenate([stack[c, z, :64], stack[c, 4 + z, :64]], axis=0).astype(F32)
            query_ref[:, m * 128 : (m + 1) * 128] = both[:, :128]
            out_ref[:, m * 128 : (m + 1) * 128] = both[:, 256:].T
        for lo, ref in ((128, key_ref), (192, value_ref)):
            for a in range(2):
                ref[a * 64 : (a + 1) * 64, z * 128 : (z + 1) * 128] = jnp.concatenate(
                    [stack[c, 4 * a + z, :64, lo : lo + 64] for c in range(2)], axis=1
                ).astype(F32)
    for a in range(2):
        gain_ref[a] = sum(stack[c, 4 * a + z, 64:].astype(F32) for c in range(2) for z in range(4))


def assemble_attention(core, same, other):
    outs = pl.pallas_call(
        assemble_attention_kernel,
        out_shape=(
            jax.ShapeDtypeStruct((TOK, D), F32),
            jax.ShapeDtypeStruct((TOK, KVH * HD), F32),
            jax.ShapeDtypeStruct((TOK, KVH * HD), F32),
            jax.ShapeDtypeStruct((TOK, D), F32),
            jax.ShapeDtypeStruct((2, 16, 384), F32),
        ),
        in_specs=[SMEM, VMEM, VMEM],
        out_specs=(VMEM,) * 5,
        scratch_shapes=[pltpu.VMEM((2, 8, 80, 384), BF16)],
        compiler_params=pltpu.CompilerParams(vmem_limit_bytes=32 * 2**20),
        cost_estimate=pl.CostEstimate(flops=0, bytes_accessed=3 * 10**6, transcendentals=0),
    )(core, same, other)
    return outs[:4] + (outs[4][:, 0, :],)


def rotate(values, cosine, sine):
    half = HD // 2
    turned = jnp.concatenate([-values[:, half:], values[:, :half]], axis=1)
    return values * cosine + turned * sine


def unrotate(grads, cosine, sine):
    half = HD // 2
    scaled = grads * sine
    turned = jnp.concatenate([scaled[:, half:], -scaled[:, :half]], axis=1)
    return grads * cosine + turned


def whole(shape):
    return pl.BlockSpec(shape, lambda i: (0,) * len(shape))


def half_rows(columns):
    return (
        pl.BlockSpec((256, columns), lambda i: (jnp.minimum(i, 1), 0)),
        pl.BlockSpec((256, columns), lambda i: (jnp.maximum(i - 2, 0), 0)),
    )


def token_rows(columns):
    return pl.BlockSpec((256, columns), lambda i: (i, 0))


def project_kernel(
    x_ref, x_other_ref, weights_ref, gain_ref, gain_query_ref, gain_key_ref, cos_ref, sin_ref,
    proj_ref, query_ref, kv_ref, w_qkv,
):
    i = pl.program_id(0)

    @pl.when(i == 0)
    def _():
        for k in range(8):
            w_qkv[k * 128 : (k + 1) * 128, :] = weights_ref[k, :128, :]

    x = jnp.where(i < 2, x_ref[...], x_other_ref[...]).astype(F32)
    h1 = (x * inv_rms(x) * gain_ref[...]).astype(BF16)
    proj = dot(h1, w_qkv[...])
    proj_ref[...] = proj
    turned = []
    for h, gain in ((0, gain_query_ref), (1, gain_query_ref), (2, gain_key_ref)):
        part = proj[:, h * HD : (h + 1) * HD]
        turned.append(rotate(part * inv_rms(part) * gain[...], cos_ref[...], sin_ref[...]).astype(BF16))
    query_ref[0] = turned[0] * jnp.asarray(HD ** -0.5, BF16)
    query_ref[1] = turned[1] * jnp.asarray(HD ** -0.5, BF16)
    kv_ref[...] = jnp.concatenate([turned[2], proj[:, 3 * HD :].astype(BF16)], axis=1)


def project(x, x_other, weights, gain, gain_query, gain_key, cosine, sine):
    first, last = half_rows(D)
    return pl.pallas_call(
        project_kernel,
        grid=(4,),
        in_specs=[
            first, last, whole((8, 144, 256)), whole((1, D)), whole((1, HD)), whole((1, HD)),
            token_rows(HD), token_rows(HD),
        ],
        out_specs=(token_rows(256), pl.BlockSpec((2, 256, HD), lambda i: (0, i, 0)), token_rows(2 * HD)),
        out_shape=(
            jax.ShapeDtypeStruct((HALF, 256), F32),
            jax.ShapeDtypeStruct((2, HALF, HD), BF16),
            jax.ShapeDtypeStruct((HALF, 2 * HD), BF16),
        ),
        scratch_shapes=[pltpu.VMEM((D, 256), BF16)],
        compiler_params=pltpu.CompilerParams(vmem_limit_bytes=32 * 2**20),
        cost_estimate=pl.CostEstimate(flops=5 * 10**8, bytes_accessed=4 * 10**6, transcendentals=0),
    )(x, x_other, weights, gain, gain_query, gain_key, cosine, sine)


def project_back_kernel(
    x_ref, x_other_ref, weights_ref, gain_ref, gain_query_ref, gain_key_ref, cos_ref, sin_ref,
    proj_ref, dq_ref, dkv_ref, dkv_peer_ref,
    mine_ref, low_ref, weight_ref, gain_grad_ref, query_grad_ref, key_grad_ref, w_qkv, total,
):
    i = pl.program_id(0)

    @pl.when(i == 0)
    def _():
        for k in range(8):
            w_qkv[k * 128 : (k + 1) * 128, :] = weights_ref[k, :128, :]
        total[...] = jnp.zeros_like(total)
        for ref in (gain_grad_ref, query_grad_ref, key_grad_ref):
            ref[...] = jnp.zeros_like(ref)

    dkv = (dkv_ref[...] + dkv_peer_ref[...].astype(F32)).astype(BF16)
    grads = (dq_ref[0], dq_ref[1], dkv[:, :HD])
    outs = []
    for h, gain, grad_ref in (
        (0, gain_query_ref, query_grad_ref),
        (1, gain_query_ref, query_grad_ref),
        (2, gain_key_ref, key_grad_ref),
    ):
        part = proj_ref[:, h * HD : (h + 1) * HD]
        scale = inv_rms(part)
        normed = part * scale
        grad = unrotate(grads[h].astype(F32), cos_ref[...], sin_ref[...])
        grad_ref[...] += jnp.sum(grad * normed, axis=0, keepdims=True)
        outs.append(norm_back(grad * gain[...], normed, scale).astype(BF16))
    dqkv = jnp.concatenate(outs + [dkv[:, HD:]], axis=1)
    x = jnp.where(i < 2, x_ref[...], x_other_ref[...]).astype(F32)
    n1 = x * inv_rms(x)
    h1 = (n1 * gain_ref[...]).astype(BF16)
    dh1 = dot(dqkv, w_qkv[...], ((1,), (1,)))
    gain_grad_ref[...] += jnp.sum(dh1 * n1, axis=0, keepdims=True)
    total[...] += dot(h1, dqkv, ((0,), (0,)))

    @pl.when(i < 2)
    def _():
        mine_ref[...] = dh1

    @pl.when(i >= 2)
    def _():
        low_ref[...] = dh1.astype(BF16)

    @pl.when(i == 3)
    def _():
        weight_ref[...] = total[...].astype(BF16)


def project_back(x, x_other, weights, gain, gain_query, gain_key, cosine, sine, proj, dq, dkv, dkv_peer):
    first, last = half_rows(D)
    return pl.pallas_call(
        project_back_kernel,
        grid=(4,),
        in_specs=[
            first, last, whole((8, 144, 256)), whole((1, D)), whole((1, HD)), whole((1, HD)),
            token_rows(HD), token_rows(HD), token_rows(256),
            pl.BlockSpec((2, 256, HD), lambda i: (0, i, 0)), token_rows(2 * HD), token_rows(2 * HD),
        ],
        out_specs=(first, last, whole((D, 256)), whole((1, D)), whole((1, HD)), whole((1, HD))),
        out_shape=(
            jax.ShapeDtypeStruct((512, D), F32),
            jax.ShapeDtypeStruct((512, D), BF16),
            jax.ShapeDtypeStruct((D, 256), BF16),
            jax.ShapeDtypeStruct((1, D), F32),
            jax.ShapeDtypeStruct((1, HD), F32),
            jax.ShapeDtypeStruct((1, HD), F32),
        ),
        scratch_shapes=[pltpu.VMEM((D, 256), BF16), pltpu.VMEM((D, 256), F32)],
        compiler_params=pltpu.CompilerParams(vmem_limit_bytes=32 * 2**20),
        cost_estimate=pl.CostEstimate(flops=10**9, bytes_accessed=6 * 10**6, transcendentals=0),
    )(x, x_other, weights, gain, gain_query, gain_key, cosine, sine, proj, dq, dkv, dkv_peer)


def inv_rms(values):
    return lax.rsqrt(jnp.mean(values * values, axis=-1, keepdims=True) + EPS)


def norm_back(grads, normed, scale):
    return scale * (grads - normed * jnp.mean(grads * normed, axis=-1, keepdims=True))


def per_device(
    tokens, cotangent, places, doc_split,
    w_query, w_key, w_value, w_out, w_gate, w_up, w_down,
    norm_attn, norm_ffn, norm_query, norm_key,
):
    a, z, c = lax.axis_index("a"), lax.axis_index("z"), lax.axis_index("c")
    m = z * 2 + c
    own_tokens, own_cot = tokens[0], cotangent[0]

    gains = jnp.concatenate([norm_attn, norm_ffn, norm_query, norm_key, jnp.zeros((240,), BF16)])
    gains = jnp.concatenate([gains.reshape(2, 256), jnp.zeros((14, 256), BF16)], axis=0)
    qkv_own = jnp.concatenate(
        [
            lax.dynamic_slice_in_dim(w_query, m * 128, 128, 1),
            lax.dynamic_slice_in_dim(w_key, m * 64, 64, 1),
            lax.dynamic_slice_in_dim(w_value, m * 64, 64, 1),
        ],
        axis=1,
    )
    qkv_own = jnp.concatenate([qkv_own, gains], axis=0)
    qkv_all = lax.all_to_all(
        jnp.broadcast_to(qkv_own[None], (8, 144, 256)), FS, split_axis=0, concat_axis=0, tiled=True
    )
    w_down_m = fetch_shard(w_down)
    x_same = ring(own_tokens)
    x_other = swap(x_same, "c")
    gain_parts = qkv_all[:, 128:130].reshape(8, 512).astype(F32)
    gain_attn = gain_parts[:, :128].reshape(D)
    gain_ffn = gain_parts[:, 128:256].reshape(D)
    gain_query = gain_parts[:, 256:264].reshape(HD)
    gain_key = gain_parts[:, 264:272].reshape(HD)

    wide_own = jnp.concatenate(
        [
            w_out,
            lax.dynamic_slice_in_dim(w_gate, m * FSL, FSL, 1),
            jnp.zeros((TOK, 64), BF16),
            lax.dynamic_slice_in_dim(w_up, m * FSL, FSL, 1),
        ],
        axis=1,
    )
    wide = lax.all_gather(wide_own, FS, axis=0)

    block_of = places[0].reshape(32, BLK)[:, 0] // BLK
    wanted = []
    for half in (a, 1 - a):
        for dc in range(2):
            for dz in range(4):
                device = half * 8 + ((z - dz) % 4) * 2 + (c ^ dc)
                wanted += [device * 2, device * 2 + 1]
    wanted = jnp.stack(wanted)
    blocks = jnp.sum(
        jnp.where(wanted[:, None] == jnp.arange(32)[None, :], block_of[None, :], 0), axis=1
    ).astype(jnp.int32)
    place = (blocks[:16, None] * BLK + jnp.arange(BLK)[None, :]).reshape(HALF)
    split = doc_split[0]
    position = (place - jnp.where(place >= split, split, 0)).astype(F32)
    inv_freq = THETA ** (-2.0 * jnp.arange(HD // 2).astype(F32) / HD)
    phases = position[:, None] * inv_freq[None, :]
    phases = jnp.concatenate([phases, phases], axis=-1)
    cosine, sine = jnp.cos(phases), jnp.sin(phases)

    tables = (gain_attn[None], gain_query[None], gain_key[None], cosine, sine)
    proj, q_scaled, kv_own = project(x_same, x_other, qkv_all, *tables)
    kv_peer = swap(kv_own, "a")
    cot_same = ring(after(own_cot, kv_own))
    attended, sums = attention_forward(blocks, doc_split, q_scaled, kv_own, kv_peer)

    heads_same = heads_ring(attended)
    heads_same, cot_same, w_down_m = after((heads_same, cot_same, w_down_m))
    heads_other = swap(heads_same, "c")
    cot_other = swap(cot_same, "c")
    order = jnp.stack(
        [((z - dz) % 4) * 2 + (c ^ dc) for dc in range(2) for dz in range(4)]
    ).astype(jnp.int32)
    h2, d_gate, d_up, act, dh2_mine, dh2_low, out_mine, out_low, own_y1, grad_gain_ffn = ffn(
        order, x_same, x_other, heads_same, heads_other, wide, w_down_m, cot_same, cot_other, gain_ffn[None]
    )

    dh2_same = add_cores(dh2_mine, dh2_low)
    ffn_terms = ffn_weights(h2, cot_same, cot_other, d_gate, d_up, act)
    ffn_got = lax.all_to_all(ffn_terms, ("y", "b", "a"), split_axis=0, concat_axis=0, tiled=True)
    dh2 = add_ring(dh2_same, ffn_terms)
    own_r2 = inv_rms(own_y1)
    own_n2 = own_y1 * own_r2
    dy1 = own_cot.astype(F32) + norm_back(dh2 * gain_ffn, own_n2, own_r2)
    dz_low = dy1.astype(BF16)
    dz_same = ring(dz_low)
    dz_other = swap(dz_same, "c")
    out_same = add_cores(out_mine, after(out_low, dz_same))

    w_out_m = lax.dynamic_index_in_dim(wide, m, 0, keepdims=False)[:, :D]
    d_att = jnp.concatenate(
        [dot(part, w_out_m, ((1,), (1,))).astype(BF16) for part in (dz_same, dz_other)], axis=0
    )
    dq_rot, dkv_own, dkv_peer = attention_backward(
        blocks, doc_split, q_scaled, kv_own, kv_peer, attended, d_att, sums
    )
    layer_out = (own_y1 + add_ring(out_same)).astype(BF16)
    dkv_peer = swap(dkv_peer, "a")
    ffn_piece = jnp.sum(after(ffn_got, dq_rot).astype(F32), axis=0).astype(BF16)
    ffn_piece = jnp.concatenate([ffn_piece[:2], cross(ffn_piece[2])[None]], axis=0)
    dkv_peer, ffn_piece = after((dkv_peer, ffn_piece))
    ffn_all = lax.all_gather(ffn_piece, CTX, axis=0).reshape(2, 8, 3, 64, FSL)
    out_terms = dot(dz_same, attended[:512], ((0,), (0,))) + dot(dz_other, attended[512:], ((0,), (0,)))
    dh1_mine, dh1_low, qkv_terms, grad_gain_attn, grad_gain_query, grad_gain_key = project_back(
        x_same, x_other, qkv_all, *tables, proj, dq_rot, dkv_own, dkv_peer
    )

    attn_terms = jnp.concatenate([qkv_terms, out_terms.astype(BF16)], axis=1)
    gain_terms = jnp.concatenate(
        [
            grad_gain_attn.reshape(8, 128),
            grad_gain_ffn.reshape(8, 128),
            grad_gain_query.reshape(8, 8),
            grad_gain_key.reshape(8, 8),
        ],
        axis=1,
    ).reshape(8, 2, 1, 136)
    gain_terms = jnp.pad(gain_terms, ((0, 0), (0, 0), (0, 15), (0, 384 - 136)))
    terms = jnp.concatenate([attn_terms.reshape(8, 2, 64, 384), gain_terms.astype(BF16)], axis=2)
    terms = terms.reshape(16, 80, 384)
    dh1_same = add_cores(dh1_mine, dh1_low, terms)
    dh1 = add_ring(dh1_same)
    own_x = own_tokens.astype(F32)
    own_r1 = inv_rms(own_x)
    grad_tokens = (dy1 + norm_back(dh1 * gain_attn, own_x * own_r1, own_r1)).astype(BF16)
    got = lax.all_to_all(terms, ("y", "b", "a"), split_axis=0, concat_axis=0, tiled=True)
    piece = jnp.sum(after(got, dh1_same).astype(F32), axis=0).astype(BF16)
    piece = jnp.concatenate([piece[:, :256], cross(piece[:, 256:])], axis=1)
    piece, grad_tokens = after((piece, grad_tokens))
    ffn_grads = assemble_ffn(ffn_all)
    piece, ffn_grads, layer_out = after((piece, ffn_grads, layer_out))
    grad_gate, grad_up, grad_down = ffn_grads
    same = lax.all_to_all(
        jnp.broadcast_to(piece[None], (8, 80, 384)), ("a", "z"), split_axis=0, concat_axis=0, tiled=True
    )
    first_core = jnp.full((1,), c, jnp.int32)
    grad_query, grad_key, grad_value, grad_out, gain_sum = assemble_attention(
        first_core, same, swap(same, "c")
    )
    gain_sum = gain_sum[:, :136].reshape(272)
    return (
        layer_out[None],
        grad_tokens[None],
        grad_query,
        grad_key,
        grad_value,
        grad_out,
        grad_gate,
        grad_up,
        grad_down,
        gain_sum[:128],
        gain_sum[128:256],
        gain_sum[256:264],
        gain_sum[264:],
    )


def solution(mesh):
    fine = Mesh(mesh.devices.reshape(NA, NZ, NC, NY, NB), CTX + FS)
    rows = P(FS, CTX, None)
    shard = P(FS, None)
    in_specs = (rows, rows, shard, P(FS)) + (shard,) * 7 + (P(FS),) * 4
    out_specs = (rows, rows) + (shard,) * 7 + (P(FS),) * 4
    return jax.shard_map(
        per_device, mesh=fine, in_specs=in_specs, out_specs=out_specs, check_vma=False
    )
```
